32 devices in a mesh: dp: 8 (over y, x, core), tensor: 4 (over z).
Axes of the slice: x: 2, y: 2, z: 4, core: 2. Of those that a mesh axis runs over, the one named last changes fastest.
Arguments:
- residual: bfloat16 [128, 7168], P('dp'), may hold values from -6 to 6
- query_latent: bfloat16 [128, 128, 512], P('dp', 'tensor'), may hold values from -64 to 64
- query_rope: bfloat16 [128, 128, 64], P('dp', 'tensor'), may hold values from -6 to 6
- cache_latent: bfloat16 [128, 1024, 512], P('dp'), may hold values from -4 to 4
- cache_rope: bfloat16 [128, 64, 1024], P('dp'), may hold values from -6 to 6
- lengths: int32 [128], P('dp'), may hold values from 256 to 1024, as said below
- value_up: bfloat16 [128, 512, 128], P('tensor'), may hold values from -0.25 to 0.25
- out_proj: bfloat16 [16384, 7168], P('tensor', 'dp'), may hold values from -0.5 to 0.5
- gate_proj: bfloat16 [8, 7168, 1024], P('dp', None, 'tensor'), may hold values from -0.0625 to 0.0625
- up_proj: bfloat16 [8, 7168, 1024], P('dp', None, 'tensor'), may hold values from -0.0625 to 0.0625
- down_proj: bfloat16 [8, 1024, 7168], P('dp', 'tensor'), may hold values from -0.1875 to 0.1875
- groups: int32 [128, 4], P('dp'), may hold values from 0 to 3, as said below
- expert_picks: int32 [128, 8], P('dp'), may hold values from 0 to 7, as said below
- gate_levels: int32 [128, 8], P('dp'), may hold values from 1 to 255
Outputs:
- layer_out: bfloat16 [128, 7168], P('dp')
The draws below stay inside these ranges and needn't reach their ends.
Inputs may be any that keep to these rules, and one draw needn't show every extreme that they name: Row r attends to cache positions 0 to lengths[r] - 1; in every draw some row has length 1024. Each row names 4 different groups; among the rows of one index of dp no group is named by more than 16 rows. `expert_picks`: each row's 8 entries differ, so its experts differ. Among the rows of one index of dp no expert is named by more than 16 rows; in every draw one expert is named by exactly 16 rows of every index of dp.
All inputs are finite; a program needn't handle non-finite values.
Results may differ from the reference program's by a relative error of at most 0.02.
Values may be sent and summed in bfloat16 or wider, within the bound.
A program may use at most 128 MiB of HBM per device.

```python
import jax
import jax.numpy as jnp
from jax import lax

D = 7168
HEADS = 128
LAT = 512
ROPE = 64
V_HEAD = 128
FF = 1024
TOPK = 8
TOPG = 4
B_DEV = 16
S = 1024
ROWS = 128
EXPERTS = 8
GROUPS = 4
EPG = 2


def draw_query_latent(key, part):
    key = jax.random.fold_in(key, 3)
    base_key = jax.random.fold_in(key, 0)
    values = jax.random.truncated_normal(base_key, -4.0, 4.0, (ROWS, HEADS, LAT), jnp.float32)
    return values.astype(jnp.bfloat16)


def draw_cache_latent(key, part):
    key = jax.random.fold_in(key, 5)
    values = jax.random.truncated_normal(key, -4.0, 4.0, (ROWS, S, LAT), jnp.float32)
    return values.astype(jnp.bfloat16)


def draw_lengths(key, part):
    key = jax.random.fold_in(key, 9)
    draw_key, place_key = jax.random.split(key)
    lengths_drawn = jax.random.randint(draw_key, (ROWS,), S // 4, S + 1)
    longest = jax.random.randint(place_key, (), 0, ROWS)
    return jnp.where(jnp.arange(ROWS) == longest, S, lengths_drawn).astype(jnp.int32)


def draw_routing(key):
    hot_key, perm_key, start_key, order_key, pick_key, shuffle_key = jax.random.split(key, 6)
    hot_expert = jax.random.randint(hot_key, (), 0, EXPERTS)
    hot_group = hot_expert // EPG
    blocks = ROWS // B_DEV
    group_range = jnp.arange(GROUPS, dtype=jnp.int32)
    group_score = jax.random.randint(perm_key, (blocks, GROUPS), 0, 4096) * GROUPS + group_range[None, :]
    group_score = jnp.where(group_range[None, :] == hot_group, -1, group_score)
    ranked = jnp.argsort(group_score, axis=1).astype(jnp.int32)
    layout = jnp.roll(ranked, TOPG - 1, axis=1)
    starts = jax.vmap(lambda block_key: jax.random.permutation(block_key, B_DEV))(jax.random.split(start_key, blocks))
    positions = (starts[:, :, None].astype(jnp.int32) + jnp.arange(TOPG, dtype=jnp.int32)[None, None, :]) % GROUPS
    chosen = jnp.take_along_axis(jnp.broadcast_to(layout[:, None, :], (blocks, B_DEV, GROUPS)), positions, axis=2)
    chosen = chosen.reshape(ROWS, TOPG)
    order_score = jax.random.randint(order_key, (ROWS, TOPG), 0, 4096) * TOPG + jnp.arange(TOPG, dtype=jnp.int32)[None, :]
    groups = jnp.take_along_axis(chosen, jnp.argsort(order_score, axis=1), axis=1)
    present = jnp.any(groups == hot_group, axis=1)
    hot_slot = jnp.argmax(groups == hot_group, axis=1).astype(jnp.int32)
    width_all = TOPG * EPG
    candidate_ids = jnp.arange(width_all, dtype=jnp.int32)
    hot_candidate = hot_slot * EPG + hot_expert % EPG
    pick_score = jax.random.randint(pick_key, (ROWS, width_all), 0, 4096) * width_all + candidate_ids[None, :]
    forced = present[:, None] & (candidate_ids[None, :] == hot_candidate[:, None])
    pick_score = jnp.where(forced, 8192 * width_all, pick_score)
    unused_values, picked = lax.top_k(pick_score, TOPK)
    shuffle_score = jax.random.randint(shuffle_key, (ROWS, TOPK), 0, 4096) * TOPK + jnp.arange(TOPK, dtype=jnp.int32)[None, :]
    expert_picks = jnp.take_along_axis(picked, jnp.argsort(shuffle_score, axis=1), axis=1)
    return (groups.astype(jnp.int32), expert_picks.astype(jnp.int32))


def draw_groups(key, part):
    routed = draw_routing(key)
    return routed[0]


def draw_expert_picks(key, part):
    routed = draw_routing(key)
    return routed[1]


def plant(entries, key, least, largest):
    extent = entries.shape
    spot = [jax.random.randint(jax.random.fold_in(key, axis), (), 0, extent[axis]) for axis in range(len(extent))]
    entries = entries.at[tuple(spot)].set(least)
    longest = extent.index(max(extent))
    spot[longest] = (spot[longest] + 1) % extent[longest]
    return entries.at[tuple(spot)].set(largest)


def steps_of(rng, extent, shards, smallest, high):
    level = 1.0
    for position, shards_of in shards:
        draws = jax.random.uniform(jax.random.fold_in(jax.random.fold_in(rng, 6), position), (shards_of,), jnp.float32, smallest / len(shards), high / len(shards))
        level = level * jnp.repeat(jnp.exp(draws), extent[position] // shards_of).reshape((-1,) + (1,) * (len(extent) - 1 - position))
    return level


def noise(key, dims, deviation, most, pieces=(), held_as=jnp.bfloat16):
    loudness = steps_of(key, dims, pieces, -0.22, 0.18) if pieces else 1.0
    entries = jax.random.normal(key, dims, jnp.float32) * deviation * loudness
    return jnp.minimum(jnp.maximum(entries, -most), most).astype(held_as)


def setup_inputs(seed: int = 0) -> dict:
    seeds = jax.random.split(jax.random.key(seed), 15)
    residual = noise(seeds[0], (ROWS, D), 1.0, 6.0, ((0, 8),))
    query_latent = draw_query_latent(jax.random.fold_in(seeds[14], 71), 0)
    query_rope = noise(seeds[2], (ROWS, HEADS, ROPE), 1.0, 6.0, ((0, 8), (1, 4)))
    cache_latent = draw_cache_latent(jax.random.fold_in(seeds[14], 71), 0)
    cache_rope = noise(seeds[4], (ROWS, ROPE, S), 1.0, 6.0, ((0, 8),))
    lengths = draw_lengths(jax.random.fold_in(seeds[14], 71), 0)
    value_up = noise(seeds[6], (HEADS, LAT, V_HEAD), LAT ** -0.5, 0.25, ((0, 4),))
    out_proj = noise(seeds[7], (HEADS * V_HEAD, D), V_HEAD ** -0.5, 0.5, ((0, 4), (1, 8)))
    gate_proj = noise(seeds[8], (EXPERTS, D, FF), D ** -0.5, 0.0625, ((0, 8), (2, 4)))
    up_proj = noise(seeds[9], (EXPERTS, D, FF), D ** -0.5, 0.0625, ((0, 8), (2, 4)))
    down_proj = noise(seeds[10], (EXPERTS, FF, D), FF ** -0.5, 0.1875, ((0, 8), (1, 4)))
    groups = draw_groups(jax.random.fold_in(seeds[14], 71), 0)
    expert_picks = draw_expert_picks(jax.random.fold_in(seeds[14], 71), 0)
    gate_levels = plant(jax.random.randint(seeds[13], (ROWS, TOPK), 1, 256), jax.random.fold_in(seeds[13], 1), 1, 255).astype(jnp.int32)
    return dict(residual=residual, query_latent=query_latent, query_rope=query_rope, cache_latent=cache_latent, cache_rope=cache_rope, lengths=lengths, value_up=value_up, out_proj=out_proj, gate_proj=gate_proj, up_proj=up_proj, down_proj=down_proj, groups=groups, expert_picks=expert_picks, gate_levels=gate_levels)


score_scale = 192.0 ** -0.5
route_scale = 2.5
far_below = -1.0e30


def attend_row(operands):
    row_query, row_rope, row_cache, row_keys, row_length = operands
    scores = jnp.dot(row_query, row_cache.T, preferred_element_type=jnp.float32)
    scores = (scores + jnp.dot(row_rope, row_keys, preferred_element_type=jnp.float32)) * score_scale
    visible = jnp.arange(S) < row_length
    scores = jnp.where(visible[None, :], scores, far_below)
    highest = jnp.max(scores, axis=1, keepdims=True)
    raised = jnp.exp(scores - highest)
    weights = (raised / jnp.sum(raised, axis=1, keepdims=True)).astype(jnp.bfloat16)
    return jnp.dot(weights, row_cache, preferred_element_type=jnp.float32).astype(jnp.bfloat16)


def reference(residual, query_latent, query_rope, cache_latent, cache_rope, lengths, value_up, out_proj, gate_proj, up_proj, down_proj, groups, expert_picks, gate_levels):
    latent_mix = lax.map(attend_row, (query_latent, query_rope, cache_latent, cache_rope, lengths))
    latent_mix = lax.optimization_barrier(latent_mix)
    head_out = jnp.einsum("rhl,hlv->rhv", latent_mix.astype(jnp.float32), value_up.astype(jnp.float32)).astype(jnp.bfloat16)
    head_out = head_out.reshape(ROWS, HEADS * V_HEAD)
    attention = lax.optimization_barrier(jnp.dot(head_out, out_proj, preferred_element_type=jnp.float32).astype(jnp.bfloat16))
    hidden = (residual.astype(jnp.float32) + attention.astype(jnp.float32)).astype(jnp.bfloat16)
    hidden = lax.optimization_barrier(hidden)
    slot_group = expert_picks // EPG
    expert_ids = jnp.take_along_axis(groups, slot_group, axis=1) * EPG + expert_picks % EPG
    levels = gate_levels.astype(jnp.float32)
    gates = route_scale * levels / jnp.sum(levels, axis=1, keepdims=True)

    def one_expert(running, operands):
        expert_index, gate_weight, up_weight, down_weight = operands
        coefficient = jnp.sum(jnp.where(expert_ids == expert_index, gates, 0.0), axis=1)
        gated = jnp.dot(hidden, gate_weight, preferred_element_type=jnp.float32)
        upward = jnp.dot(hidden, up_weight, preferred_element_type=jnp.float32)
        activation = (jax.nn.silu(gated) * upward).astype(jnp.bfloat16)
        produced = lax.optimization_barrier(jnp.dot(activation, down_weight, preferred_element_type=jnp.float32).astype(jnp.bfloat16))
        return running + coefficient[:, None] * produced.astype(jnp.float32), None

    routed, unused = lax.scan(one_expert, jnp.zeros((ROWS, D), jnp.float32), (jnp.arange(EXPERTS, dtype=jnp.int32), gate_proj, up_proj, down_proj))
    return (hidden.astype(jnp.float32) + routed).astype(jnp.bfloat16)
```

```python
import functools

import jax
import jax.numpy as jnp
from jax import lax
from jax.experimental import pallas as pl
from jax.experimental.pallas import tpu as pltpu
from jax.sharding import PartitionSpec as P

score_scale = 192.0 ** (-0.5)
route_scale = 2.5
far_below = -1e30
MIB = 1 << 20
F32 = jnp.float32
BF16 = jnp.bfloat16


def attend_kernel(
    step_rows, owners, per_group, lengths, q_lat, q_rope, c_lat, c_rope, resid, groups, picks,
    levels, value_up, head_ref, resid_ref, coef_ref, mix_s, value_s, value_sem,
):
    step = pl.program_id(0)
    rows = resid.shape[0]
    heads = q_lat.shape[1]
    positions = c_lat.shape[1]
    width = value_up.shape[2]
    fetch = pltpu.make_async_copy(value_up, value_s, value_sem)

    @pl.when(step == 0)
    def _first():
        fetch.start()
        cols = resid_ref.shape[2]
        for j in range(owners):
            resid_ref[j] = resid[:, j * cols : (j + 1) * cols]
        lane = lax.broadcasted_iota(jnp.int32, coef_ref.shape, 1)
        level = levels[...].astype(F32)
        gates = route_scale * level / jnp.sum(level, axis=1, keepdims=True)
        group = groups[...]
        pick_all = picks[...]
        total = jnp.zeros(coef_ref.shape, F32)
        for k in range(pick_all.shape[1]):
            pick = pick_all[:, k : k + 1]
            expert = pick
            for s in range(group.shape[1]):
                inside = (pick >= s * per_group) & (pick < (s + 1) * per_group)
                shifted = pick + (group[:, s : s + 1] - s) * per_group
                expert = jnp.where(inside, shifted, expert)
            total += jnp.where(lane == expert, gates[:, k : k + 1], 0.0)
        coef_ref[...] = total

    for i in range(step_rows):
        row = step * step_rows + i
        scores = lax.dot_general(
            q_lat[i], c_lat[i], (((1,), (1,)), ((), ())), preferred_element_type=F32
        )
        scores += jnp.dot(q_rope[i], c_rope[i], preferred_element_type=F32)
        place = lax.broadcasted_iota(jnp.int32, (heads, positions), 1)
        scores = jnp.where(place < lengths[row], scores * score_scale, far_below)
        highest = jnp.max(scores, axis=1, keepdims=True)
        raised = jnp.exp(scores - highest)
        total = jnp.sum(raised, axis=1, keepdims=True)
        weights = (raised / total).astype(BF16)
        mix_s[row] = jnp.dot(weights, c_lat[i], preferred_element_type=F32)

    @pl.when(step == pl.num_programs(0) - 1)
    def _last():
        fetch.wait()
        for h in range(heads):
            mixed = mix_s[:, h, :].astype(BF16)
            head = jnp.dot(mixed, value_s[h], preferred_element_type=F32)
            head_ref[:, h * width : (h + 1) * width] = head.astype(BF16)


def attend(owners, per_group, residual, query_latent, query_rope, cache_latent, cache_rope,
           lengths, value_up, groups, expert_picks, gate_levels):
    rows, heads, lat = query_latent.shape
    positions = cache_latent.shape[1]
    rope = query_rope.shape[2]
    width = value_up.shape[2]
    model = residual.shape[1]
    step_rows = 2
    whole = lambda shape: pl.BlockSpec(shape, lambda i: (0,) * len(shape))
    per_step = lambda a, b: pl.BlockSpec((step_rows, a, b), lambda i: (i, 0, 0))
    return pl.pallas_call(
        functools.partial(attend_kernel, step_rows, owners, per_group),
        grid=(rows // step_rows,),
        in_specs=[
            pl.BlockSpec(memory_space=pltpu.SMEM),
            per_step(heads, lat),
            per_step(heads, rope),
            per_step(positions, lat),
            per_step(rope, positions),
            whole(residual.shape),
            whole(groups.shape),
            whole(expert_picks.shape),
            whole(gate_levels.shape),
            pl.BlockSpec(memory_space=pl.ANY),
        ],
        out_specs=[
            whole((rows, heads * width)),
            whole((owners, rows, model // owners)),
            whole((rows, 128)),
        ],
        out_shape=[
            jax.ShapeDtypeStruct((rows, heads * width), BF16),
            jax.ShapeDtypeStruct((owners, rows, model // owners), BF16),
            jax.ShapeDtypeStruct((rows, 128), F32),
        ],
        scratch_shapes=[
            pltpu.VMEM((rows, heads, lat), F32),
            pltpu.VMEM(value_up.shape, BF16),
            pltpu.SemaphoreType.DMA,
        ],
        compiler_params=pltpu.CompilerParams(vmem_limit_bytes=32 * MIB),
        cost_estimate=pl.CostEstimate(
            flops=rows * heads * positions * 1088 * 2, bytes_accessed=24 * MIB, transcendentals=0
        ),
    )(lengths, query_latent, query_rope, cache_latent, cache_rope, residual, groups,
      expert_picks, gate_levels, value_up)


def flip(index, mask, size):
    out, bit = 0, 1
    while bit < size:
        here = index // bit % 2
        out = out + bit * ((here + 1) % 2 if mask & bit else here)
        bit *= 2
    return out


def layer_kernel(
    dp, tp, head, resid, coef, wo_h, wg_h, wu_h, wd_h, hid_out, routed_out,
    wo, wg, wu, wd, hbuf, cbuf, resb, acc, pbuf, rbuf, hid, accg, accu, pd, sr, xs, xr, zs, zr, fin,
    w_sem, c_s, c_r, a_s, a_r, f_s, f_r, q_s, q_r, b_s, b_r, z_s, z_r, x_s, x_r, y_s, y_r,
    d_s, d_r, e_s, e_r, g_s, g_r, o_s, o_r,
):
    d = lax.axis_index("dp")
    t = lax.axis_index("tensor")
    chips = dp // 2
    chip, core = d // 2, d % 2
    sib = chip * 2 + (1 - core)
    row_n = head.shape[0]
    rows = dp * row_n
    quarter = rows // tp
    cols = wo.shape[1]
    depth = wo.shape[0]
    part = fin.shape[2]
    per_quarter = dp // tp
    far_first = list(range(chips - 1, 0, -1))

    def send(src, dst, ss, rs, **where):
        copy = pltpu.make_async_remote_copy(
            src_ref=src, dst_ref=dst, send_sem=ss, recv_sem=rs,
            device_id=where, device_id_type=pl.DeviceIdType.MESH,
        )
        return copy

    loads = [
        pltpu.make_async_copy(src, dst, w_sem.at[i])
        for i, (src, dst) in enumerate(((wo_h, wo), (wg_h.at[0], wg), (wu_h.at[0], wu), (wd_h.at[0], wd)))
    ]
    for load in loads:
        load.start()

    barrier = pltpu.get_barrier_semaphore()
    for k in range(1, dp):
        pl.semaphore_signal(barrier, inc=1, device_id={"dp": (d + k) % dp}, device_id_type=pl.DeviceIdType.MESH)
    for k in range(1, tp):
        pl.semaphore_signal(barrier, inc=1, device_id={"tensor": (t + k) % tp}, device_id_type=pl.DeviceIdType.MESH)
    pl.semaphore_wait(barrier, dp - 1 + tp - 1)

    pending = []

    gather = {}
    for j in far_first:
        gather[j] = send(head, hbuf.at[d], a_s.at[j], a_r.at[j], dp=flip(chip, j, chips) * 2 + core)
        gather[j].start()
    gather[0] = send(head, hbuf.at[d], a_s.at[0], a_r.at[0], dp=sib)
    gather[0].start()
    pending += gather.values()
    hbuf[d] = head[...]

    coefs = []
    for k in range(1, dp):
        coefs.append(send(coef, cbuf.at[d], c_s.at[k], c_r.at[k], dp=(d + k) % dp))
        coefs[-1].start()
    pending += coefs
    cbuf[d] = coef[...]

    mine = d // per_quarter == t
    slot = d % per_quarter
    shares = [
        send(resid.at[(d + k) % dp], resb.at[slot], q_s.at[k], q_r.at[slot], dp=(d + k) % dp)
        for k in range(1, dp)
    ]

    @pl.when(mine)
    def _share():
        for copy in shares:
            copy.start()
        resb[slot] = resid[d]

    forwards = []
    for j in range(1, chips):
        gather[j].wait_recv()
        block = flip(chip, j, chips) * 2 + core
        forwards.append(send(hbuf.at[block], hbuf.at[block], f_s.at[j], f_r.at[j], dp=sib))
        forwards[-1].start()
    pending += forwards
    loads[0].wait()
    gather[0].wait_recv()
    for copy in forwards:
        copy.wait_recv()

    acc[...] = jnp.zeros_like(acc)
    chunk = 512

    @pl.loop(0, depth // chunk)
    def _project(k):
        at = pl.ds(pl.multiple_of(k * chunk, chunk), chunk)
        acc[...] += jnp.dot(
            hbuf[:, :, at].reshape(rows, chunk), wo[at, :], preferred_element_type=F32
        )

    for u in range(tp):
        pbuf[u] = acc[u * quarter : (u + 1) * quarter, :].astype(BF16)
    sums = []
    for k in range(1, tp):
        u = (t + k) % tp
        sums.append(send(pbuf.at[u], rbuf.at[k - 1], b_s.at[k], b_r.at[k], tensor=u))
        sums[-1].start()
    pending += sums
    for i in range(per_quarter):
        owner = t * per_quarter + i

        @pl.when(owner != d)
        def _arrive():
            send(resid.at[0], resb.at[i], q_s.at[0], q_r.at[i], dp=owner).wait_recv()

    my_rows = pl.ds(pl.multiple_of(t * quarter, quarter), quarter)
    piece = acc[my_rows, :]
    for k in range(1, tp):
        sums[k - 1].wait_recv()
        piece += rbuf[k - 1].astype(F32)
    attention = piece.astype(BF16).astype(F32)
    hid[d, my_rows, :] = (attention + resb[...].reshape(quarter, cols).astype(F32)).astype(BF16)

    along = []
    for k in range(1, tp):
        along.append(send(hid.at[d, my_rows], hid.at[d, my_rows], z_s.at[k], z_r.at[k], tensor=(t + k) % tp))
        along[-1].start()
    pending += along
    spread = {}
    for k in range(tp):
        if k:
            along[k - 1].wait_recv()
        at = pl.ds(pl.multiple_of((t + tp - k) % tp * quarter, quarter), quarter)
        for j in far_first:
            spread[k, j] = send(hid.at[d, at], hid.at[d, at], x_s.at[k, j], x_r.at[k, j], dp=flip(chip, j, chips) * 2 + core)
            spread[k, j].start()
        spread[k, 0] = send(hid.at[d, at], hid.at[d, at], x_s.at[k, 0], x_r.at[k, 0], dp=sib)
        spread[k, 0].start()
    pending += spread.values()

    loads[1].wait()
    loads[2].wait()
    accg[...] = jnp.zeros_like(accg)
    accu[...] = jnp.zeros_like(accu)

    def expand(block):
        at = pl.ds(pl.multiple_of(block * cols, cols), cols)
        values = hid[block]
        accg[...] += jnp.dot(values, wg[at, :], preferred_element_type=F32)
        accu[...] += jnp.dot(values, wu[at, :], preferred_element_type=F32)

    expand(d)
    passed = {}
    for k in range(tp):
        at = pl.ds(pl.multiple_of((t + tp - k) % tp * quarter, quarter), quarter)
        for j in range(1, chips):
            spread[k, j].wait_recv()
            block = flip(chip, j, chips) * 2 + core
            passed[k, j] = send(hid.at[block, at], hid.at[block, at], y_s.at[k, j], y_r.at[k, j], dp=sib)
            passed[k, j].start()
    pending += passed.values()
    for k in range(tp):
        spread[k, 0].wait_recv()

    @pl.loop(0, chips - 1)
    def _same(j):
        expand((chip + 1 + j) % chips * 2 + core)

    expand(sib)
    for copy in passed.values():
        copy.wait_recv()

    @pl.loop(0, chips - 1)
    def _other(j):
        expand((chip + 1 + j) % chips * 2 + 1 - core)

    for copy in coefs:
        copy.wait_recv()
    table = cbuf[...].reshape(rows, 128)
    lane = lax.broadcasted_iota(jnp.int32, (rows, 128), 1)
    weight = jnp.sum(jnp.where(lane == d, table, 0.0), axis=1, keepdims=True)
    gated = accg[...]
    active = (gated / (1.0 + jnp.exp(-gated)) * accu[...] * weight).astype(BF16)

    loads[3].wait()
    order = [(t + k) % tp for k in list(range(1, tp)) + [0]]
    halves = []
    for n, c in enumerate(order):
        at = pl.ds(pl.multiple_of(c * part, part), part)
        produced = jnp.dot(active, wd[:, at], preferred_element_type=F32).astype(BF16)
        for b in range(dp):
            pd[n, b % 2, b // 2] = produced[b * row_n : (b + 1) * row_n, :]
        halves.append(send(pd.at[n, 1 - core], sr.at[n], d_s.at[n], d_r.at[n], dp=sib))
        halves[-1].start()
    pending += halves
    across = {}
    for n in range(tp):
        halves[n].wait_recv()
        xs[n] = (pd[n, core].astype(F32) + sr[n].astype(F32)).astype(BF16)
        for j in far_first:
            peer = flip(chip, j, chips)
            across[n, j] = send(xs.at[n, peer], xr.at[n, j - 1], e_s.at[n, j], e_r.at[n, j], dp=peer * 2 + core)
            across[n, j].start()
    pending += across.values()
    reduced = []
    for n in range(tp):
        total = xs[n, chip].astype(F32)
        for j in range(1, chips):
            across[n, j].wait_recv()
            total += xr[n, j - 1].astype(F32)
        if n < tp - 1:
            zs[n] = total.astype(BF16)
            reduced.append(send(zs.at[n], zr.at[n], g_s.at[n], g_r.at[n], tensor=order[n]))
            reduced[-1].start()
    pending += reduced
    for n in range(tp - 1):
        reduced[n].wait_recv()
        total += zr[n].astype(F32)
    fin[t] = total.astype(BF16)
    last = []
    for k in range(1, tp):
        last.append(send(fin.at[t], fin.at[t], o_s.at[k], o_r.at[k], tensor=(t + k) % tp))
        last[-1].start()
    pending += last
    hid_out[...] = hid[:, pl.ds(pl.multiple_of(d * row_n, row_n), row_n), :]
    for copy in last:
        copy.wait_recv()
    routed_out[...] = fin[...]
    for copy in pending:
        copy.wait_send()

    @pl.when(mine)
    def _shared():
        for copy in shares:
            copy.wait_send()


def layer(dp, tp, head, resid, coef, wo, wg, wu, wd):
    row_n = head.shape[0]
    rows = dp * row_n
    depth, cols = wo.shape
    model, units = wg.shape[1:]
    quarter = rows // tp
    part = model // tp
    chips = dp // 2
    vm = lambda *shape: pltpu.VMEM(shape, BF16)
    sem = lambda *shape: pltpu.SemaphoreType.DMA(shape)
    return pl.pallas_call(
        functools.partial(layer_kernel, dp, tp),
        out_shape=[
            jax.ShapeDtypeStruct((dp, row_n, cols), BF16),
            jax.ShapeDtypeStruct((tp, row_n, part), BF16),
        ],
        in_specs=[pl.BlockSpec(memory_space=pltpu.VMEM)] * 3 + [pl.BlockSpec(memory_space=pl.ANY)] * 4,
        out_specs=[pl.BlockSpec(memory_space=pltpu.VMEM)] * 2,
        scratch_shapes=[
            vm(depth, cols), vm(model, units), vm(model, units), vm(units, model),
            vm(dp, row_n, depth), pltpu.VMEM((dp, row_n, 128), F32), vm(dp // tp, row_n, cols),
            pltpu.VMEM((rows, cols), F32), vm(tp, quarter, cols), vm(tp - 1, quarter, cols),
            vm(dp, rows, cols), pltpu.VMEM((rows, units), F32), pltpu.VMEM((rows, units), F32),
            vm(tp, 2, chips, row_n, part), vm(tp, chips, row_n, part), vm(tp, chips, row_n, part),
            vm(tp, chips - 1, row_n, part), vm(tp - 1, row_n, part), vm(tp - 1, row_n, part),
            vm(tp, row_n, part),
            sem(4), sem(dp), sem(dp), sem(chips), sem(chips), sem(chips), sem(chips),
            sem(dp), sem(dp // tp), sem(tp), sem(tp), sem(tp), sem(tp),
            sem(tp, chips), sem(tp, chips), sem(tp, chips), sem(tp, chips),
            sem(tp), sem(tp), sem(tp, chips), sem(tp, chips), sem(tp), sem(tp), sem(tp), sem(tp),
        ],
        compiler_params=pltpu.CompilerParams(
            collective_id=0, has_side_effects=True, vmem_limit_bytes=56 * MIB
        ),
        cost_estimate=pl.CostEstimate(
            flops=2 * rows * (depth * cols + 3 * model * units),
            bytes_accessed=20 * MIB, transcendentals=0,
        ),
    )(head, resid, coef, wo, wg, wu, wd)


def local(
    dp, tp, residual, query_latent, query_rope, cache_latent, cache_rope, lengths, value_up, out_proj,
    gate_proj, up_proj, down_proj, groups, expert_picks, gate_levels,
):
    rows, model = residual.shape
    per_group = dp // min(8, dp // 2)
    head, resid, coef = attend(
        dp, per_group, residual, query_latent, query_rope, cache_latent, cache_rope, lengths,
        value_up, groups, expert_picks, gate_levels,
    )
    hidden, routed = layer(dp, tp, head, resid, coef, out_proj, gate_proj, up_proj, down_proj)
    hidden = jnp.transpose(hidden, (1, 0, 2)).reshape(rows, model)
    routed = jnp.transpose(routed, (1, 0, 2)).reshape(rows, model)
    return (hidden.astype(F32) + routed.astype(F32)).astype(BF16)


def solution(mesh):
    return jax.shard_map(
        functools.partial(local, mesh.shape["dp"], mesh.shape["tensor"]),
        mesh=mesh,
        in_specs=(
            P("dp", None),
            P("dp", "tensor", None),
            P("dp", "tensor", None),
            P("dp", None, None),
            P("dp", None, None),
            P("dp"),
            P("tensor", None, None),
            P("tensor", "dp"),
            P("dp", None, "tensor"),
            P("dp", None, "tensor"),
            P("dp", "tensor", None),
            P("dp", None),
            P("dp", None),
            P("dp", None),
        ),
        out_specs=P("dp", None),
        check_vma=False,
    )
```

```python
import functools

import jax
import jax.numpy as jnp
from jax import lax
from jax.experimental import pallas as pl
from jax.experimental.pallas import tpu as pltpu
from jax.sharding import PartitionSpec as P

score_scale = 192.0 ** (-0.5)
route_scale = 2.5
far_below = -1e30
MIB = 1 << 20
F32 = jnp.float32
BF16 = jnp.bfloat16


def flip(index, mask, size):
    out, bit = 0, 1
    while bit < size:
        here = index // bit % 2
        out = out + bit * ((here + 1) % 2 if mask & bit else here)
        bit *= 2
    return out


def gate_table(owners, per_group, groups, picks, levels):
    rows = picks.shape[1]
    level = levels[...].astype(F32)
    gates = route_scale * level / jnp.sum(level, axis=0, keepdims=True)
    group = groups[...]
    pick = picks[...]
    expert = pick
    for s in range(group.shape[0]):
        inside = (pick >= s * per_group) & (pick < (s + 1) * per_group)
        expert = jnp.where(inside, pick + (group[s : s + 1, :] - s) * per_group, expert)
    same = lax.broadcasted_iota(jnp.int32, (rows, rows), 0) == lax.broadcasted_iota(jnp.int32, (rows, rows), 1)
    lane = lax.broadcasted_iota(jnp.int32, (rows, 128), 1)
    total = jnp.zeros((rows, 128), F32)
    for e in range(owners):
        along = jnp.sum(jnp.where(expert == e, gates, 0.0), axis=0, keepdims=True)
        down = jnp.sum(jnp.where(same, along, 0.0), axis=1, keepdims=True)
        total += jnp.where(lane == e, down, 0.0)
    return total


def layer_kernel(
    dp, tp, per_group, lengths, resid, groups, picks, levels,
    ql_h, qr_h, cl_h, cr_h, vu_h, wo_h, wg_h, wu_h, wd_h, out,
    ql, qr, cl, cr, vu, mix, wo, wg, wu, wd, rblk, head, hbuf, cbuf, resb, acc, pbuf, rbuf, hid,
    accg, accu, pd, sr, xr, zs, zr, fin, hcat,
    l_sem, r_sem, w_sem, c_s, c_r, a_s, a_r, f_s, f_r, q_s, q_r, b_s, b_r, z_s, z_r, x_s, x_r, y_s, y_r,
    d_s, d_r, e_s, e_r, g_s, g_r, o_s, o_r,
):
    d = lax.axis_index("dp")
    t = lax.axis_index("tensor")
    chips = dp // 2
    chip, core = d // 2, d % 2
    sib = chip * 2 + (1 - core)
    row_n = resid.shape[0]
    rows = dp * row_n
    quarter = rows // tp
    depth, cols = wo.shape
    per_quarter = dp // tp
    cpq = chips // tp
    near_first = list(range(1, chips))
    far_first = near_first[::-1]
    steps = row_n // cl.shape[1]
    step_rows = cl.shape[1]
    heads, positions = ql.shape[1], cl.shape[2]
    width = vu.shape[2]

    def send(src, dst, ss, rs, **where):
        return pltpu.make_async_remote_copy(
            src_ref=src, dst_ref=dst, send_sem=ss, recv_sem=rs,
            device_id=where, device_id_type=pl.DeviceIdType.MESH,
        )

    def over(mask):
        return flip(chip, mask, chips) * 2 + core

    barrier = pltpu.get_barrier_semaphore()
    for k in range(1, dp):
        pl.semaphore_signal(barrier, inc=1, device_id={"dp": (d + k) % dp}, device_id_type=pl.DeviceIdType.MESH)
    for k in range(1, tp):
        pl.semaphore_signal(barrier, inc=1, device_id={"tensor": (t + k) % tp}, device_id_type=pl.DeviceIdType.MESH)

    def fetch(step, slot):
        at = pl.ds(step * step_rows, step_rows)
        return (
            pltpu.make_async_copy(cl_h.at[at], cl.at[slot], l_sem.at[slot]),
            pltpu.make_async_copy(cr_h.at[at], cr.at[slot], r_sem.at[slot]),
        )

    loads = [
        pltpu.make_async_copy(src, dst, w_sem.at[i])
        for i, (src, dst) in enumerate((
            (wo_h, wo), (wg_h.at[0], wg), (wu_h.at[0], wu), (wd_h.at[0], wd), (vu_h, vu), (ql_h, ql), (qr_h, qr),
        ))
    ]
    loads[5].start()
    loads[6].start()
    for copy in fetch(0, 0):
        copy.start()
    for j in range(dp):
        rblk[j] = resid[:, j * cols : (j + 1) * cols]
    cbuf[d] = gate_table(dp, per_group, groups, picks, levels)
    loads[5].wait()
    loads[6].wait()

    @pl.loop(0, steps)
    def _attend(step):
        slot = step % 2

        @pl.when(step + 1 < steps)
        def _next():
            for copy in fetch(step + 1, 1 - slot):
                copy.start()

        @pl.when(step == 0)
        def _later():
            loads[4].start()
            loads[0].start()

        @pl.when(step == 1)
        def _latest():
            for i in (1, 2, 3):
                loads[i].start()

        for copy in fetch(step, slot):
            copy.wait()
        place = lax.broadcasted_iota(jnp.int32, (heads, positions), 1)
        base = step * step_rows
        span = range(step_rows)
        scores = [
            lax.dot_general(ql[base + i], cl[slot, i], (((1,), (1,)), ((), ())), preferred_element_type=F32)
            + jnp.dot(qr[base + i], cr[slot, i], preferred_element_type=F32)
            for i in span
        ]
        scores = [jnp.where(place < lengths[base + i], scores[i] * score_scale, far_below) for i in span]
        highest = [jnp.max(scores[i], axis=1, keepdims=True) for i in span]
        raised = [jnp.exp(scores[i] - highest[i]) for i in span]
        totals = [jnp.sum(raised[i], axis=1, keepdims=True) for i in span]
        for i in span:
            mix[base + i] = jnp.dot(raised[i].astype(BF16), cl[slot, i], preferred_element_type=F32) / totals[i]

    pl.semaphore_wait(barrier, dp - 1 + tp - 1)
    pending = []

    coefs = []
    for k in range(1, dp):
        coefs.append(send(cbuf.at[d], cbuf.at[d], c_s.at[k], c_r.at[k], dp=(d + k) % dp))
        coefs[-1].start()
    pending += coefs

    mine = d // per_quarter == t
    slot = d % per_quarter
    shares = [
        send(rblk.at[(d + k) % dp], resb.at[slot], q_s.at[k], q_r.at[slot], dp=(d + k) % dp)
        for k in range(1, dp)
    ]

    @pl.when(mine)
    def _share():
        for copy in shares:
            copy.start()
        resb[slot] = rblk[d]

    loads[4].wait()
    for h in range(heads):
        mixed = mix[:, h, :].astype(BF16)
        value = jnp.dot(mixed, vu[h], preferred_element_type=F32)
        head[:, h * width : (h + 1) * width] = value.astype(BF16)

    gather = {0: send(head, hbuf.at[d], a_s.at[0], a_r.at[0], dp=sib)}
    for j in near_first:
        gather[j] = send(head, hbuf.at[d], a_s.at[j], a_r.at[j], dp=over(j))
    for j in near_first + [0]:
        gather[j].start()
    pending += gather.values()
    hbuf[d] = head[...]
    loads[0].wait()

    forwards = {}

    def pass_on(m):
        for j in range(m * cpq, (m + 1) * cpq):
            if j:
                gather[j].wait_recv()
                block = over(j)
                forwards[j] = send(hbuf.at[block], hbuf.at[block], f_s.at[j], f_r.at[j], dp=sib)
                forwards[j].start()

    chunk = 1024
    sums = []
    pass_on(0)
    for m in range(tp):
        for j in range(m * cpq, (m + 1) * cpq):
            (forwards[j] if j else gather[0]).wait_recv()
        if m >= 1 and m + 1 < tp:
            pass_on(m + 1)
        which = flip(chip // cpq, m, tp)
        blocks = pl.ds(which * per_quarter, per_quarter)
        acc[which] = jnp.zeros((quarter, cols), F32)

        @pl.loop(0, depth // chunk)
        def _project(k):
            at = pl.ds(pl.multiple_of(k * chunk, chunk), chunk)
            acc[which] += jnp.dot(
                hbuf[blocks, :, at].reshape(quarter, chunk), wo[at, :], preferred_element_type=F32
            )

        if m == 0 and tp > 1:
            pass_on(1)
        pbuf[which] = acc[which].astype(BF16)
        place = (which - t + tp) % tp

        @pl.when(which != t)
        def _sum():
            send(pbuf.at[which], rbuf.at[place], b_s.at[m], b_r.at[place], tensor=which).start()

        sums.append((which, place))
    pending += forwards.values()
    for i in range(per_quarter):
        owner = t * per_quarter + i

        @pl.when(owner != d)
        def _arrive():
            send(rblk.at[0], resb.at[i], q_s.at[0], q_r.at[i], dp=owner).wait_recv()

    my_rows = pl.ds(pl.multiple_of(t * quarter, quarter), quarter)
    piece = acc[t]
    for k in range(1, tp):
        send(pbuf.at[0], rbuf.at[k], b_s.at[0], b_r.at[k], tensor=(t + k) % tp).wait_recv()
        piece += rbuf[k].astype(F32)
    attention = piece.astype(BF16).astype(F32)
    hid[d, my_rows, :] = (attention + resb[...].reshape(quarter, cols).astype(F32)).astype(BF16)

    along = []
    for k in range(1, tp):
        along.append(send(hid.at[d, my_rows], hid.at[d, my_rows], z_s.at[k], z_r.at[k], tensor=(t + k) % tp))
        along[-1].start()
    pending += along
    spread = {}
    for k in range(tp):
        if k:
            along[k - 1].wait_recv()
        at = pl.ds(pl.multiple_of((t + tp - k) % tp * quarter, quarter), quarter)
        for j in near_first:
            spread[k, j] = send(hid.at[d, at], hid.at[d, at], x_s.at[k, j], x_r.at[k, j], dp=over(j))
            spread[k, j].start()
        spread[k, 0] = send(hid.at[d, at], hid.at[d, at], x_s.at[k, 0], x_r.at[k, 0], dp=sib)
        spread[k, 0].start()
    pending += spread.values()

    loads[1].wait()
    loads[2].wait()
    accg[...] = jnp.zeros_like(accg)
    accu[...] = jnp.zeros_like(accu)

    def expand(block):
        at = pl.ds(pl.multiple_of(block * cols, cols), cols)
        values = hid[block]
        accg[...] += jnp.dot(values, wg[at, :], preferred_element_type=F32)
        accu[...] += jnp.dot(values, wu[at, :], preferred_element_type=F32)

    expand(d)
    passed = {}
    for k in range(tp):
        at = pl.ds(pl.multiple_of((t + tp - k) % tp * quarter, quarter), quarter)
        for j in near_first:
            spread[k, j].wait_recv()
            block = over(j)
            passed[k, j] = send(hid.at[block, at], hid.at[block, at], y_s.at[k, j], y_r.at[k, j], dp=sib)
            passed[k, j].start()
    pending += passed.values()
    for k in range(tp):
        spread[k, 0].wait_recv()

    @pl.loop(0, chips - 1)
    def _same(j):
        expand((chip + 1 + j) % chips * 2 + core)

    expand(sib)
    for copy in passed.values():
        copy.wait_recv()

    @pl.loop(0, chips - 1)
    def _other(j):
        expand((chip + 1 + j) % chips * 2 + 1 - core)

    for copy in coefs:
        copy.wait_recv()
    table = cbuf[...].reshape(rows, 128)
    lane = lax.broadcasted_iota(jnp.int32, (rows, 128), 1)
    weight = jnp.sum(jnp.where(lane == d, table, 0.0), axis=1, keepdims=True)
    gated = accg[...]
    active = (gated / (1.0 + jnp.exp(-gated)) * accu[...] * weight).astype(BF16)

    loads[3].wait()
    split, part = fin.shape[1], fin.shape[3]
    pieces = [(s, k) for s in range(split) for k in list(range(1, tp)) + [0]]
    halves = []
    for n, (s, k) in enumerate(pieces):
        at = pl.ds(pl.multiple_of(((t + k) % tp * split + s) * part, part), part)
        produced = jnp.dot(active, wd[:, at], preferred_element_type=F32).astype(BF16)
        for b in range(dp):
            pd[n, b % 2, b // 2] = produced[b * row_n : (b + 1) * row_n, :]
        halves.append(send(pd.at[n, 1 - core], sr.at[n], d_s.at[n], d_r.at[n], dp=sib))
        halves[-1].start()
    pending += halves
    across = {}
    for n in range(len(pieces)):
        halves[n].wait_recv()
        pd[n, core] = (pd[n, core].astype(F32) + sr[n].astype(F32)).astype(BF16)
        for j in far_first:
            peer = flip(chip, j, chips)
            across[n, j] = send(pd.at[n, core, peer], xr.at[n, j - 1], e_s.at[n, j], e_r.at[n, j], dp=peer * 2 + core)
            across[n, j].start()
    pending += across.values()
    own_rows = pl.ds(pl.multiple_of(d * row_n, row_n), row_n)
    reduced = {}
    last = []
    for n, (s, k) in enumerate(pieces):
        total = pd[n, core, chip].astype(F32)
        for j in far_first:
            across[n, j].wait_recv()
            total += xr[n, j - 1].astype(F32)
        if k:
            zs[n] = total.astype(BF16)
            reduced[s, k] = send(zs.at[n], zr.at[n], g_s.at[n], g_r.at[n], tensor=(t + k) % tp)
            reduced[s, k].start()
        else:
            first = (t * split + s) * part // cols
            for i in range(part // cols):
                hcat[:, i * cols : (i + 1) * cols] = hid[first + i, own_rows, :].astype(F32)
            for m in range(1, tp):
                reduced[s, m].wait_recv()
                total += zr[s * tp + m - 1].astype(F32)
            fin[t, s] = (hcat[...] + total).astype(BF16)
            for m in range(1, tp):
                last.append(send(fin.at[t, s], fin.at[t, s], o_s.at[s, m], o_r.at[s, m], tensor=(t + m) % tp))
                last[-1].start()
    pending += reduced.values()
    pending += last
    for copy in last:
        copy.wait_recv()
    for c in range(tp):
        for s in range(split):
            out[:, (c * split + s) * part : (c * split + s + 1) * part] = fin[c, s]
    for copy in pending:
        copy.wait_send()
    for m, (which, place) in enumerate(sums):

        @pl.when(which != t)
        def _summed():
            send(pbuf.at[which], rbuf.at[place], b_s.at[m], b_r.at[place], tensor=which).wait_send()

    @pl.when(mine)
    def _shared():
        for copy in shares:
            copy.wait_send()


def local(
    dp, tp, residual, query_latent, query_rope, cache_latent, cache_rope, lengths, value_up, out_proj,
    gate_proj, up_proj, down_proj, groups, expert_picks, gate_levels,
):
    row_n, model = residual.shape
    per_group = dp // min(8, dp // 2)
    rows = dp * row_n
    depth, cols = out_proj.shape
    units = gate_proj.shape[2]
    heads, lat = query_latent.shape[1:]
    quarter = rows // tp
    split = 2
    part = model // (tp * split)
    count = tp * split
    chips = dp // 2
    step_rows = 4
    vm = lambda *shape: pltpu.VMEM(shape, BF16)
    wide = lambda *shape: pltpu.VMEM(shape, F32)
    sem = lambda *shape: pltpu.SemaphoreType.DMA(shape)
    return pl.pallas_call(
        functools.partial(layer_kernel, dp, tp, per_group),
        out_shape=jax.ShapeDtypeStruct((row_n, model), BF16),
        in_specs=[pl.BlockSpec(memory_space=pltpu.SMEM)]
        + [pl.BlockSpec(memory_space=pltpu.VMEM)] * 4
        + [pl.BlockSpec(memory_space=pl.ANY)] * 9,
        out_specs=pl.BlockSpec(memory_space=pltpu.VMEM),
        scratch_shapes=[
            vm(*query_latent.shape), vm(*query_rope.shape),
            vm(2, step_rows, *cache_latent.shape[1:]), vm(2, step_rows, *cache_rope.shape[1:]),
            vm(*value_up.shape), wide(row_n, heads, lat),
            vm(depth, cols), vm(model, units), vm(model, units), vm(units, model),
            vm(dp, row_n, cols), vm(row_n, depth), vm(dp, row_n, depth), wide(dp, row_n, 128),
            vm(dp // tp, row_n, cols),
            wide(tp, quarter, cols), vm(tp, quarter, cols), vm(tp, quarter, cols),
            vm(dp, rows, cols), wide(rows, units), wide(rows, units),
            vm(count, 2, chips, row_n, part), vm(count, chips, row_n, part),
            vm(count, chips - 1, row_n, part), vm(count, row_n, part), vm(count, row_n, part),
            vm(tp, split, row_n, part), wide(row_n, part),
            sem(2), sem(2), sem(7), sem(dp), sem(dp), sem(chips), sem(chips), sem(chips), sem(chips),
            sem(dp), sem(dp // tp), sem(tp), sem(tp), sem(tp), sem(tp),
            sem(tp, chips), sem(tp, chips), sem(tp, chips), sem(tp, chips),
            sem(count), sem(count), sem(count, chips), sem(count, chips), sem(count), sem(count),
            sem(split, tp), sem(split, tp),
        ],
        compiler_params=pltpu.CompilerParams(
            collective_id=0, has_side_effects=True, vmem_limit_bytes=60 * MIB
        ),
        cost_estimate=pl.CostEstimate(
            flops=2 * rows * (depth * cols + 3 * model * units) + 2 * row_n * heads * 1024 * 1088,
            bytes_accessed=42 * MIB, transcendentals=0,
        ),
    )(
        lengths, residual, groups.T, expert_picks.T, gate_levels.T, query_latent, query_rope,
        cache_latent, cache_rope, value_up, out_proj, gate_proj, up_proj, down_proj,
    )


def solution(mesh):
    return jax.shard_map(
        functools.partial(local, mesh.shape["dp"], mesh.shape["tensor"]),
        mesh=mesh,
        in_specs=(
            P("dp", None),
            P("dp", "tensor", None),
            P("dp", "tensor", None),
            P("dp", None, None),
            P("dp", None, None),
            P("dp"),
            P("tensor", None, None),
            P("tensor", "dp"),
            P("dp", None, "tensor"),
            P("dp", None, "tensor"),
            P("dp", "tensor", None),
            P("dp", None),
            P("dp", None),
            P("dp", None),
        ),
        out_specs=P("dp", None),
        check_vma=False,
    )
```

```python
import functools

import jax
import jax.numpy as jnp
from jax import lax
from jax.experimental import pallas as pl
from jax.experimental.pallas import tpu as pltpu
from jax.sharding import PartitionSpec as P

score_scale = 192.0 ** (-0.5)
route_scale = 2.5
far_below = -1e30
MIB = 1 << 20
F32 = jnp.float32
BF16 = jnp.bfloat16


def flip(index, mask, size):
    out, bit = 0, 1
    while bit < size:
        here = index // bit % 2
        out = out + bit * ((here + 1) % 2 if mask & bit else here)
        bit *= 2
    return out


def gate_table(owners, per_group, groups, picks, levels):
    rows = picks.shape[1]
    level = levels[...].astype(F32)
    gates = route_scale * level / jnp.sum(level, axis=0, keepdims=True)
    group = groups[...]
    pick = picks[...]
    expert = pick
    for s in range(group.shape[0]):
        inside = (pick >= s * per_group) & (pick < (s + 1) * per_group)
        expert = jnp.where(inside, pick + (group[s : s + 1, :] - s) * per_group, expert)
    same = lax.broadcasted_iota(jnp.int32, (rows, rows), 0) == lax.broadcasted_iota(jnp.int32, (rows, rows), 1)
    lane = lax.broadcasted_iota(jnp.int32, (rows, 128), 1)
    total = jnp.zeros((rows, 128), F32)
    for e in range(owners):
        along = jnp.sum(jnp.where(expert == e, gates, 0.0), axis=0, keepdims=True)
        down = jnp.sum(jnp.where(same, along, 0.0), axis=1, keepdims=True)
        total += jnp.where(lane == e, down, 0.0)
    return total


def layer_kernel(
    dp, tp, per_group, lengths, resid, groups, picks, levels,
    ql_h, qr_h, cl_h, cr_h, vu_h, wo_h, wg_h, wu_h, wd_h, hid_out, out,
    ql, qr, cl, cr, vu, mix, wo, wg, wu, wd, rblk, hbuf, cbuf, resb, acc, pbuf, rbuf, hid,
    accg, accu, pd, sr, xr, zs, zr, fin,
    l_sem, r_sem, w_sem, c_s, c_r, a_s, a_r, f_s, f_r, q_s, q_r, b_s, b_r, z_s, z_r, x_s, x_r, y_s, y_r,
    d_s, d_r, e_s, e_r, g_s, g_r, o_s, o_r,
):
    d = lax.axis_index("dp")
    t = lax.axis_index("tensor")
    chips = dp // 2
    chip, core = d // 2, d % 2
    sib = chip * 2 + (1 - core)
    row_n = resid.shape[0]
    rows = dp * row_n
    quarter = rows // tp
    depth, cols = wo.shape
    per_quarter = dp // tp
    near_first = list(range(1, chips))
    far_first = near_first[::-1]
    steps = row_n // cl.shape[1]
    step_rows = cl.shape[1]
    heads, positions = ql.shape[1], cl.shape[2]
    width = vu.shape[2]
    rope = qr.shape[2]
    parts = hbuf.shape[0]
    chunk = depth // parts

    def send(src, dst, ss, rs, **where):
        return pltpu.make_async_remote_copy(
            src_ref=src, dst_ref=dst, send_sem=ss, recv_sem=rs,
            device_id=where, device_id_type=pl.DeviceIdType.MESH,
        )

    def over(mask):
        return flip(chip, mask, chips) * 2 + core

    barrier = pltpu.get_barrier_semaphore()
    for k in range(1, dp):
        pl.semaphore_signal(barrier, inc=1, device_id={"dp": (d + k) % dp}, device_id_type=pl.DeviceIdType.MESH)
    for k in range(1, tp):
        pl.semaphore_signal(barrier, inc=1, device_id={"tensor": (t + k) % tp}, device_id_type=pl.DeviceIdType.MESH)

    def fetch(step, slot):
        at = pl.ds(step * step_rows, step_rows)
        return (
            pltpu.make_async_copy(cl_h.at[at], cl.at[slot], l_sem.at[slot]),
            pltpu.make_async_copy(cr_h.at[at], cr.at[slot], r_sem.at[slot]),
        )

    loads = [
        pltpu.make_async_copy(src, dst, w_sem.at[i])
        for i, (src, dst) in enumerate((
            (wo_h, wo), (wg_h.at[0], wg), (wu_h.at[0], wu), (wd_h.at[0], wd), (vu_h, vu), (ql_h, ql), (qr_h, qr),
        ))
    ]
    loads[5].start()
    loads[6].start()
    for copy in fetch(0, 0):
        copy.start()
    for j in range(dp):
        rblk[j] = resid[:, j * cols : (j + 1) * cols]
    cbuf[d] = gate_table(dp, per_group, groups, picks, levels)
    loads[5].wait()
    loads[6].wait()

    @pl.loop(0, steps)
    def _attend(step):
        slot = step % 2

        @pl.when(step + 1 < steps)
        def _next():
            for copy in fetch(step + 1, 1 - slot):
                copy.start()

        @pl.when(step == 0)
        def _later():
            loads[4].start()
            loads[0].start()

        @pl.when(step == 1)
        def _latest():
            for i in (1, 2, 3):
                loads[i].start()

        for copy in fetch(step, slot):
            copy.wait()
        place = lax.broadcasted_iota(jnp.int32, (heads, positions), 1)
        base = step * step_rows
        span = range(step_rows)
        ropes = qr[pl.ds(base, step_rows)].reshape(step_rows * heads, rope)
        spread_q = jnp.concatenate([ropes] * step_rows, axis=1)
        from_row = lax.broadcasted_iota(jnp.int32, spread_q.shape, 0) // heads
        to_row = lax.broadcasted_iota(jnp.int32, spread_q.shape, 1) // rope
        spread_q = jnp.where(from_row == to_row, spread_q.astype(F32), 0.0).astype(BF16)
        keys = cr[slot].reshape(step_rows * rope, positions)
        rope_scores = jnp.dot(spread_q, keys, preferred_element_type=F32)
        scores = [
            lax.dot_general(ql[base + i], cl[slot, i], (((1,), (1,)), ((), ())), preferred_element_type=F32)
            + rope_scores[i * heads : (i + 1) * heads, :]
            for i in span
        ]
        scores = [jnp.where(place < lengths[base + i], scores[i] * score_scale, far_below) for i in span]
        highest = [jnp.max(scores[i], axis=1, keepdims=True) for i in span]
        raised = [jnp.exp(scores[i] - highest[i]) for i in span]
        totals = [jnp.sum(raised[i], axis=1, keepdims=True) for i in span]
        for i in span:
            mix[base + i] = jnp.dot(raised[i].astype(BF16), cl[slot, i], preferred_element_type=F32) / totals[i]

    pl.semaphore_wait(barrier, dp - 1 + tp - 1)
    pending = []

    coefs = []
    for k in range(1, dp):
        coefs.append(send(cbuf.at[d], cbuf.at[d], c_s.at[k], c_r.at[k], dp=(d + k) % dp))
        coefs[-1].start()
    pending += coefs

    mine = d // per_quarter == t
    slot = d % per_quarter
    shares = [
        send(rblk.at[(d + k) % dp], resb.at[slot], q_s.at[k], q_r.at[slot], dp=(d + k) % dp)
        for k in range(1, dp)
    ]

    @pl.when(mine)
    def _share():
        for copy in shares:
            copy.start()
        resb[slot] = rblk[d]

    loads[4].wait()
    gather = {}
    for p in range(parts):
        for h in range(p * heads // parts, (p + 1) * heads // parts, 2):
            mixed = jnp.concatenate([mix[:, h, :], mix[:, h + 1, :]], axis=0).astype(BF16)
            both = jnp.concatenate([vu[h], vu[h + 1]], axis=1)
            value = jnp.dot(mixed, both, preferred_element_type=F32).astype(BF16)
            at = h * width - p * chunk
            hbuf[p, d, :, at : at + width] = value[:row_n, :width]
            hbuf[p, d, :, at + width : at + 2 * width] = value[row_n:, width:]
        block = hbuf.at[p, d]
        for j in near_first + [0]:
            gather[p, j] = send(block, block, a_s.at[p, j], a_r.at[p, j], dp=over(j) if j else sib)
            gather[p, j].start()
    pending += gather.values()
    loads[0].wait()

    forwards = {}
    for p in range(parts):
        for j in near_first:
            gather[p, j].wait_recv()
            block = hbuf.at[p, over(j)]
            forwards[p, j] = send(block, block, f_s.at[p, j], f_r.at[p, j], dp=sib)
            forwards[p, j].start()
        gather[p, 0].wait_recv()
        for j in near_first:
            forwards[p, j].wait_recv()
        fine = min(512, chunk)
        if p == 0:
            acc[...] = jnp.zeros_like(acc)

        @pl.loop(0, chunk // fine)
        def _project(k):
            at = pl.ds(pl.multiple_of(k * fine, fine), fine)
            down = pl.ds(pl.multiple_of(p * chunk + k * fine, fine), fine)
            acc[...] += jnp.dot(
                hbuf[p, :, :, at].reshape(rows, fine), wo[down, :], preferred_element_type=F32
            ).reshape(acc.shape)

    pending += forwards.values()
    pbuf[...] = acc[...].astype(BF16)
    sums = []
    for k in range(1, tp):
        u = (t + k) % tp
        sums.append(send(pbuf.at[u], rbuf.at[k], b_s.at[k], b_r.at[k], tensor=u))
        sums[-1].start()
    pending += sums
    for i in range(per_quarter):
        owner = t * per_quarter + i

        @pl.when(owner != d)
        def _arrive():
            send(rblk.at[0], resb.at[i], q_s.at[0], q_r.at[i], dp=owner).wait_recv()

    my_rows = pl.ds(pl.multiple_of(t * quarter, quarter), quarter)
    piece = acc[t]
    for k in range(1, tp):
        sums[k - 1].wait_recv()
        piece += rbuf[k].astype(F32)
    attention = piece.astype(BF16).astype(F32)
    hid[d, my_rows, :] = (attention + resb[...].reshape(quarter, cols).astype(F32)).astype(BF16)

    along = []
    for k in range(1, tp):
        along.append(send(hid.at[d, my_rows], hid.at[d, my_rows], z_s.at[k], z_r.at[k], tensor=(t + k) % tp))
        along[-1].start()
    pending += along
    spread = {}
    for k in range(tp):
        if k:
            along[k - 1].wait_recv()
        at = pl.ds(pl.multiple_of((t + tp - k) % tp * quarter, quarter), quarter)
        for j in near_first:
            spread[k, j] = send(hid.at[d, at], hid.at[d, at], x_s.at[k, j], x_r.at[k, j], dp=over(j))
            spread[k, j].start()
        spread[k, 0] = send(hid.at[d, at], hid.at[d, at], x_s.at[k, 0], x_r.at[k, 0], dp=sib)
        spread[k, 0].start()
    pending += spread.values()

    loads[1].wait()
    loads[2].wait()
    accg[...] = jnp.zeros_like(accg)
    accu[...] = jnp.zeros_like(accu)

    def expand(block):
        at = pl.ds(pl.multiple_of(block * cols, cols), cols)
        values = hid[block]
        accg[...] += jnp.dot(values, wg[at, :], preferred_element_type=F32)
        accu[...] += jnp.dot(values, wu[at, :], preferred_element_type=F32)

    expand(d)
    passed = {}
    for k in range(tp):
        if k == tp - 1:
            for m in range(tp):
                spread[m, 0].wait_recv()
            expand(sib)
        at = pl.ds(pl.multiple_of((t + tp - k) % tp * quarter, quarter), quarter)
        for j in near_first:
            spread[k, j].wait_recv()
            block = over(j)
            passed[k, j] = send(hid.at[block, at], hid.at[block, at], y_s.at[k, j], y_r.at[k, j], dp=sib)
            passed[k, j].start()
    pending += passed.values()

    @pl.loop(0, chips - 1)
    def _same(j):
        expand((chip + 1 + j) % chips * 2 + core)

    for copy in passed.values():
        copy.wait_recv()

    @pl.loop(0, chips - 1)
    def _other(j):
        expand((chip + 1 + j) % chips * 2 + 1 - core)

    for copy in coefs:
        copy.wait_recv()
    table = cbuf[...].reshape(rows, 128)
    lane = lax.broadcasted_iota(jnp.int32, (rows, 128), 1)
    weight = jnp.sum(jnp.where(lane == d, table, 0.0), axis=1, keepdims=True)
    gated = accg[...]
    active = (gated / (1.0 + jnp.exp(-gated)) * accu[...] * weight).astype(BF16)

    loads[3].wait()
    split, part = fin.shape[1], fin.shape[3]
    pieces = [(s, k) for s in range(split) for k in list(range(1, tp)) + [0]]
    halves = []
    across = {}

    def cross(n):
        halves[n].wait_recv()
        pd[n, core] = (pd[n, core].astype(F32) + sr[n].astype(F32)).astype(BF16)
        for j in far_first:
            peer = flip(chip, j, chips)
            across[n, j] = send(pd.at[n, core, peer], xr.at[n, j - 1], e_s.at[n, j], e_r.at[n, j], dp=peer * 2 + core)
            across[n, j].start()

    for n, (s, k) in enumerate(pieces):
        at = pl.ds(pl.multiple_of(((t + k) % tp * split + s) * part, part), part)
        produced = jnp.dot(active, wd[:, at], preferred_element_type=F32).astype(BF16)
        for b in range(dp):
            pd[n, b % 2, b // 2] = produced[b * row_n : (b + 1) * row_n, :]
        halves.append(send(pd.at[n, 1 - core], sr.at[n], d_s.at[n], d_r.at[n], dp=sib))
        halves[-1].start()
        if n >= 2:
            cross(n - 2)
    cross(len(pieces) - 2)
    cross(len(pieces) - 1)
    pending += halves
    pending += across.values()
    own_rows = pl.ds(pl.multiple_of(d * row_n, row_n), row_n)
    for b in range(dp):
        hid_out[:, b * cols : (b + 1) * cols] = hid[b, own_rows, :]
    reduced = {}
    last = []
    for n, (s, k) in enumerate(pieces):
        total = pd[n, core, chip].astype(F32)
        for j in far_first:
            across[n, j].wait_recv()
            total += xr[n, j - 1].astype(F32)
        if k:
            zs[n] = total.astype(BF16)
            reduced[s, k] = send(zs.at[n], zr.at[n], g_s.at[n], g_r.at[n], tensor=(t + k) % tp)
            reduced[s, k].start()
        else:
            for m in range(1, tp):
                reduced[s, m].wait_recv()
                total += zr[s * tp + m - 1].astype(F32)
            fin[t, s] = total.astype(BF16)
            for m in range(1, tp):
                last.append(send(fin.at[t, s], fin.at[t, s], o_s.at[s, m], o_r.at[s, m], tensor=(t + m) % tp))
                last[-1].start()
    pending += reduced.values()
    pending += last
    for copy in last:
        copy.wait_recv()
    for c in range(tp):
        for s in range(split):
            out[:, (c * split + s) * part : (c * split + s + 1) * part] = fin[c, s]
    for copy in pending:
        copy.wait_send()

    @pl.when(mine)
    def _shared():
        for copy in shares:
            copy.wait_send()


def local(
    dp, tp, residual, query_latent, query_rope, cache_latent, cache_rope, lengths, value_up, out_proj,
    gate_proj, up_proj, down_proj, groups, expert_picks, gate_levels,
):
    row_n, model = residual.shape
    per_group = dp // min(8, dp // 2)
    rows = dp * row_n
    depth, cols = out_proj.shape
    units = gate_proj.shape[2]
    heads, lat = query_latent.shape[1:]
    quarter = rows // tp
    split = 2
    part = model // (tp * split)
    count = tp * split
    chips = dp // 2
    step_rows = 4
    vm = lambda *shape: pltpu.VMEM(shape, BF16)
    wide = lambda *shape: pltpu.VMEM(shape, F32)
    sem = lambda *shape: pltpu.SemaphoreType.DMA(shape)
    hidden, routed = pl.pallas_call(
        functools.partial(layer_kernel, dp, tp, per_group),
        out_shape=[jax.ShapeDtypeStruct((row_n, model), BF16)] * 2,
        in_specs=[pl.BlockSpec(memory_space=pltpu.SMEM)]
        + [pl.BlockSpec(memory_space=pltpu.VMEM)] * 4
        + [pl.BlockSpec(memory_space=pl.ANY)] * 9,
        out_specs=[pl.BlockSpec(memory_space=pltpu.VMEM)] * 2,
        scratch_shapes=[
            vm(*query_latent.shape), vm(*query_rope.shape),
            vm(2, step_rows, *cache_latent.shape[1:]), vm(2, step_rows, *cache_rope.shape[1:]),
            vm(*value_up.shape), wide(row_n, heads, lat),
            vm(depth, cols), vm(model, units), vm(model, units), vm(units, model),
            vm(dp, row_n, cols), vm(2, dp, row_n, depth // 2), wide(dp, row_n, 128),
            vm(dp // tp, row_n, cols),
            wide(tp, quarter, cols), vm(tp, quarter, cols), vm(tp, quarter, cols),
            vm(dp, rows, cols), wide(rows, units), wide(rows, units),
            vm(count, 2, chips, row_n, part), vm(count, chips, row_n, part),
            vm(count, chips - 1, row_n, part), vm(count, row_n, part), vm(count, row_n, part),
            vm(tp, split, row_n, part),
            sem(2), sem(2), sem(7), sem(dp), sem(dp), sem(2, chips), sem(2, chips), sem(2, chips), sem(2, chips),
            sem(dp), sem(dp // tp), sem(tp), sem(tp), sem(tp), sem(tp),
            sem(tp, chips), sem(tp, chips), sem(tp, chips), sem(tp, chips),
            sem(count), sem(count), sem(count, chips), sem(count, chips), sem(count), sem(count),
            sem(split, tp), sem(split, tp),
        ],
        compiler_params=pltpu.CompilerParams(
            collective_id=0, has_side_effects=True, vmem_limit_bytes=60 * MIB
        ),
        cost_estimate=pl.CostEstimate(
            flops=2 * rows * (depth * cols + 3 * model * units) + 2 * row_n * heads * 1024 * 1088,
            bytes_accessed=42 * MIB, transcendentals=0,
        ),
    )(
        lengths, residual, groups.T, expert_picks.T, gate_levels.T, query_latent, query_rope,
        cache_latent, cache_rope, value_up, out_proj, gate_proj, up_proj, down_proj,
    )
    return (hidden.astype(F32) + routed.astype(F32)).astype(BF16)


def solution(mesh):
    return jax.shard_map(
        functools.partial(local, mesh.shape["dp"], mesh.shape["tensor"]),
        mesh=mesh,
        in_specs=(
            P("dp", None),
            P("dp", "tensor", None),
            P("dp", "tensor", None),
            P("dp", None, None),
            P("dp", None, None),
            P("dp"),
            P("tensor", None, None),
            P("tensor", "dp"),
            P("dp", None, "tensor"),
            P("dp", None, "tensor"),
            P("dp", "tensor", None),
            P("dp", None),
            P("dp", None),
            P("dp", None),
        ),
        out_specs=P("dp", None),
        check_vma=False,
    )
```

```python
import functools

import jax
import jax.numpy as jnp
from jax import lax
from jax.experimental import pallas as pl
from jax.experimental.pallas import tpu as pltpu
from jax.sharding import PartitionSpec as P

score_scale = 192.0 ** (-0.5)
route_scale = 2.5
far_below = -1e30
MIB = 1 << 20
F32 = jnp.float32
BF16 = jnp.bfloat16


def flip(index, mask, size):
    out, bit = 0, 1
    while bit < size:
        here = index // bit % 2
        out = out + bit * ((here + 1) % 2 if mask & bit else here)
        bit *= 2
    return out


def gate_table(owners, per_group, groups, picks, levels):
    rows = picks.shape[1]
    level = levels[...].astype(F32)
    gates = route_scale * level / jnp.sum(level, axis=0, keepdims=True)
    group = groups[...]
    pick = picks[...]
    expert = pick
    for s in range(group.shape[0]):
        inside = (pick >= s * per_group) & (pick < (s + 1) * per_group)
        expert = jnp.where(inside, pick + (group[s : s + 1, :] - s) * per_group, expert)
    same = lax.broadcasted_iota(jnp.int32, (rows, rows), 0) == lax.broadcasted_iota(jnp.int32, (rows, rows), 1)
    lane = lax.broadcasted_iota(jnp.int32, (rows, 128), 1)
    total = jnp.zeros((rows, 128), F32)
    for e in range(owners):
        along = jnp.sum(jnp.where(expert == e, gates, 0.0), axis=0, keepdims=True)
        down = jnp.sum(jnp.where(same, along, 0.0), axis=1, keepdims=True)
        total += jnp.where(lane == e, down, 0.0)
    return total


def layer_kernel(
    dp, tp, per_group, lengths, resid, groups, picks, levels,
    ql_h, qr_h, cl_h, cr_h, vu_h, wo_h, wg_h, wu_h, wd_h, hid_out, out,
    ql, qr, cl, cr, vu, mix, wo, wg, wu, wd, rblk, hbuf, cbuf, resb, acc, pbuf, rbuf, hid,
    accg, accu, pd, sr, xr, zs, zr, fin,
    l_sem, r_sem, w_sem, c_s, c_r, a_s, a_r, f_s, f_r, q_s, q_r, b_s, b_r, z_s, z_r, x_s, x_r, y_s, y_r,
    d_s, d_r, e_s, e_r, g_s, g_r, o_s, o_r,
):
    d = lax.axis_index("dp")
    t = lax.axis_index("tensor")
    chips = dp // 2
    chip, core = d // 2, d % 2
    sib = chip * 2 + (1 - core)
    row_n = resid.shape[0]
    rows = dp * row_n
    quarter = rows // tp
    depth, cols = wo.shape
    per_quarter = dp // tp
    near_first = list(range(1, chips))
    far_first = near_first[::-1]
    steps = row_n // cl.shape[1]
    step_rows = cl.shape[1]
    heads, positions = ql.shape[1], cl.shape[2]
    width = vu.shape[2]
    lat, rope = ql.shape[2], qr.shape[2]
    parts = hbuf.shape[0]
    chunk = depth // parts

    def send(src, dst, ss, rs, **where):
        return pltpu.make_async_remote_copy(
            src_ref=src, dst_ref=dst, send_sem=ss, recv_sem=rs,
            device_id=where, device_id_type=pl.DeviceIdType.MESH,
        )

    def over(mask):
        return flip(chip, mask, chips) * 2 + core

    barrier = pltpu.get_barrier_semaphore()
    for k in range(1, dp):
        pl.semaphore_signal(barrier, inc=1, device_id={"dp": (d + k) % dp}, device_id_type=pl.DeviceIdType.MESH)
    for k in range(1, tp):
        pl.semaphore_signal(barrier, inc=1, device_id={"tensor": (t + k) % tp}, device_id_type=pl.DeviceIdType.MESH)

    def fetch(step, slot):
        at = pl.ds(step * step_rows, step_rows)
        return (
            pltpu.make_async_copy(cl_h.at[at], cl.at[slot], l_sem.at[slot]),
            pltpu.make_async_copy(cr_h.at[at], cr.at[slot], r_sem.at[slot]),
        )

    loads = [
        pltpu.make_async_copy(src, dst, w_sem.at[i])
        for i, (src, dst) in enumerate((
            (wo_h, wo), (wg_h.at[0], wg), (wu_h.at[0], wu), (wd_h.at[0], wd), (vu_h, vu), (ql_h, ql), (qr_h, qr),
        ))
    ]
    loads[5].start()
    loads[6].start()
    for copy in fetch(0, 0):
        copy.start()
    for j in range(dp):
        rblk[j] = resid[:, j * cols : (j + 1) * cols]
    cbuf[d] = gate_table(dp, per_group, groups, picks, levels)
    loads[5].wait()
    loads[6].wait()

    @pl.loop(0, steps)
    def _attend(step):
        slot = step % 2

        @pl.when(step + 1 < steps)
        def _next():
            for copy in fetch(step + 1, 1 - slot):
                copy.start()

        @pl.when(step == 0)
        def _later():
            loads[4].start()
            loads[0].start()

        @pl.when(step == 1)
        def _latest():
            for i in (1, 2, 3):
                loads[i].start()

        for copy in fetch(step, slot):
            copy.wait()
        base = step * step_rows
        lanes = step_rows * heads

        def diagonal(queries, times):
            tiled = jnp.concatenate([queries] * times, axis=1)
            from_row = lax.broadcasted_iota(jnp.int32, tiled.shape, 0) // heads
            to_row = lax.broadcasted_iota(jnp.int32, tiled.shape, 1) // queries.shape[1]
            return jnp.where(from_row == to_row, tiled.astype(F32), 0.0).astype(BF16)

        latents = jnp.concatenate([cl[slot, i] for i in range(step_rows)], axis=1)
        q_lat = diagonal(ql[pl.ds(base, step_rows)].reshape(lanes, lat), step_rows)
        q_rope = diagonal(qr[pl.ds(base, step_rows)].reshape(lanes, rope), step_rows)
        keys = cr[slot].reshape(step_rows * rope, positions)
        scores = lax.dot_general(latents, q_lat, (((1,), (1,)), ((), ())), preferred_element_type=F32)
        scores += lax.dot_general(keys, q_rope, (((0,), (1,)), ((), ())), preferred_element_type=F32)
        lane_row = lax.broadcasted_iota(jnp.int32, (1, lanes), 1) // heads
        limit = jnp.zeros((1, lanes), jnp.int32)
        for i in range(step_rows):
            limit = jnp.where(lane_row == i, lengths[base + i], limit)
        place = lax.broadcasted_iota(jnp.int32, (positions, lanes), 0)
        scores = jnp.where(place < limit, scores * score_scale, far_below)
        raised = jnp.exp(scores - jnp.max(scores, axis=0, keepdims=True))
        weights = raised * (1.0 / jnp.sum(raised, axis=0, keepdims=True))
        weights = jnp.transpose(weights).astype(BF16)
        for i in range(step_rows):
            mix[base + i] = jnp.dot(
                weights[i * heads : (i + 1) * heads, :], cl[slot, i], preferred_element_type=F32
            )

    pl.semaphore_wait(barrier, dp - 1 + tp - 1)
    pending = []

    coefs = []
    for k in range(1, dp):
        coefs.append(send(cbuf.at[d], cbuf.at[d], c_s.at[k], c_r.at[k], dp=(d + k) % dp))
        coefs[-1].start()
    pending += coefs

    mine = d // per_quarter == t
    slot = d % per_quarter
    shares = [
        send(rblk.at[(d + k) % dp], resb.at[slot], q_s.at[k], q_r.at[slot], dp=(d + k) % dp)
        for k in range(1, dp)
    ]

    @pl.when(mine)
    def _share():
        for copy in shares:
            copy.start()
        resb[slot] = rblk[d]

    loads[4].wait()
    gather = {}
    for p in range(parts):
        for h in range(p * heads // parts, (p + 1) * heads // parts, 2):
            mixed = jnp.concatenate([mix[:, h, :], mix[:, h + 1, :]], axis=0).astype(BF16)
            both = jnp.concatenate([vu[h], vu[h + 1]], axis=1)
            value = jnp.dot(mixed, both, preferred_element_type=F32).astype(BF16)
            at = h * width - p * chunk
            hbuf[p, d, :, at : at + width] = value[:row_n, :width]
            hbuf[p, d, :, at + width : at + 2 * width] = value[row_n:, width:]
        block = hbuf.at[p, d]
        for j in near_first + [0]:
            gather[p, j] = send(block, block, a_s.at[p, j], a_r.at[p, j], dp=over(j) if j else sib)
            gather[p, j].start()
    pending += gather.values()
    loads[0].wait()

    forwards = {}
    for p in range(parts):
        for j in near_first:
            gather[p, j].wait_recv()
            block = hbuf.at[p, over(j)]
            forwards[p, j] = send(block, block, f_s.at[p, j], f_r.at[p, j], dp=sib)
            forwards[p, j].start()
        gather[p, 0].wait_recv()
        for j in near_first:
            forwards[p, j].wait_recv()
        fine = min(512, chunk)
        if p == 0:
            acc[...] = jnp.zeros_like(acc)

        @pl.loop(0, chunk // fine)
        def _project(k):
            at = pl.ds(pl.multiple_of(k * fine, fine), fine)
            down = pl.ds(pl.multiple_of(p * chunk + k * fine, fine), fine)
            acc[...] += jnp.dot(
                hbuf[p, :, :, at].reshape(rows, fine), wo[down, :], preferred_element_type=F32
            ).reshape(acc.shape)

    pending += forwards.values()
    pbuf[...] = acc[...].astype(BF16)
    sums = []
    for k in range(1, tp):
        u = (t + k) % tp
        sums.append(send(pbuf.at[u], rbuf.at[k], b_s.at[k], b_r.at[k], tensor=u))
        sums[-1].start()
    pending += sums
    for i in range(per_quarter):
        owner = t * per_quarter + i

        @pl.when(owner != d)
        def _arrive():
            send(rblk.at[0], resb.at[i], q_s.at[0], q_r.at[i], dp=owner).wait_recv()

    my_rows = pl.ds(pl.multiple_of(t * quarter, quarter), quarter)
    piece = acc[t]
    for k in range(1, tp):
        sums[k - 1].wait_recv()
        piece += rbuf[k].astype(F32)
    attention = piece.astype(BF16).astype(F32)
    hid[d, my_rows, :] = (attention + resb[...].reshape(quarter, cols).astype(F32)).astype(BF16)

    along = []
    for k in range(1, tp):
        along.append(send(hid.at[d, my_rows], hid.at[d, my_rows], z_s.at[k], z_r.at[k], tensor=(t + k) % tp))
        along[-1].start()
    pending += along
    spread = {}
    for k in range(tp):
        if k:
            along[k - 1].wait_recv()
        at = pl.ds(pl.multiple_of((t + tp - k) % tp * quarter, quarter), quarter)
        for j in near_first:
            spread[k, j] = send(hid.at[d, at], hid.at[d, at], x_s.at[k, j], x_r.at[k, j], dp=over(j))
            spread[k, j].start()
        spread[k, 0] = send(hid.at[d, at], hid.at[d, at], x_s.at[k, 0], x_r.at[k, 0], dp=sib)
        spread[k, 0].start()
    pending += spread.values()

    loads[1].wait()
    loads[2].wait()
    accg[...] = jnp.zeros_like(accg)
    accu[...] = jnp.zeros_like(accu)

    def expand(block):
        at = pl.ds(pl.multiple_of(block * cols, cols), cols)
        values = hid[block]
        accg[...] += jnp.dot(values, wg[at, :], preferred_element_type=F32)
        accu[...] += jnp.dot(values, wu[at, :], preferred_element_type=F32)

    expand(d)
    passed = {}
    for k in range(tp):
        if k == tp - 1:
            for m in range(tp):
                spread[m, 0].wait_recv()
            expand(sib)
        at = pl.ds(pl.multiple_of((t + tp - k) % tp * quarter, quarter), quarter)
        for j in near_first:
            spread[k, j].wait_recv()
            block = over(j)
            passed[k, j] = send(hid.at[block, at], hid.at[block, at], y_s.at[k, j], y_r.at[k, j], dp=sib)
            passed[k, j].start()
    pending += passed.values()

    @pl.loop(0, chips - 1)
    def _same(j):
        expand((chip + 1 + j) % chips * 2 + core)

    for copy in passed.values():
        copy.wait_recv()

    @pl.loop(0, chips - 1)
    def _other(j):
        expand((chip + 1 + j) % chips * 2 + 1 - core)

    for copy in coefs:
        copy.wait_recv()
    table = cbuf[...].reshape(rows, 128)
    lane = lax.broadcasted_iota(jnp.int32, (rows, 128), 1)
    weight = jnp.sum(jnp.where(lane == d, table, 0.0), axis=1, keepdims=True)
    gated = accg[...]
    active = (gated / (1.0 + jnp.exp(-gated)) * accu[...] * weight).astype(BF16)

    loads[3].wait()
    split, part = fin.shape[1], fin.shape[3]
    pieces = [(s, k) for s in range(split) for k in list(range(1, tp)) + [0]]
    halves = []
    across = {}

    def cross(n):
        halves[n].wait_recv()
        pd[n, core] = (pd[n, core].astype(F32) + sr[n].astype(F32)).astype(BF16)
        for j in far_first:
            peer = flip(chip, j, chips)
            across[n, j] = send(pd.at[n, core, peer], xr.at[n, j - 1], e_s.at[n, j], e_r.at[n, j], dp=peer * 2 + core)
            across[n, j].start()

    for n, (s, k) in enumerate(pieces):
        at = pl.ds(pl.multiple_of(((t + k) % tp * split + s) * part, part), part)
        produced = jnp.dot(active, wd[:, at], preferred_element_type=F32).astype(BF16)
        for b in range(dp):
            pd[n, b % 2, b // 2] = produced[b * row_n : (b + 1) * row_n, :]
        halves.append(send(pd.at[n, 1 - core], sr.at[n], d_s.at[n], d_r.at[n], dp=sib))
        halves[-1].start()
        if n >= 2:
            cross(n - 2)
    cross(len(pieces) - 2)
    cross(len(pieces) - 1)
    pending += halves
    pending += across.values()
    own_rows = pl.ds(pl.multiple_of(d * row_n, row_n), row_n)
    for b in range(dp):
        hid_out[:, b * cols : (b + 1) * cols] = hid[b, own_rows, :]
    reduced = {}
    last = []
    for n, (s, k) in enumerate(pieces):
        total = pd[n, core, chip].astype(F32)
        for j in far_first:
            across[n, j].wait_recv()
            total += xr[n, j - 1].astype(F32)
        if k:
            zs[n] = total.astype(BF16)
            reduced[s, k] = send(zs.at[n], zr.at[n], g_s.at[n], g_r.at[n], tensor=(t + k) % tp)
            reduced[s, k].start()
        else:
            for m in range(1, tp):
                reduced[s, m].wait_recv()
                total += zr[s * tp + m - 1].astype(F32)
            fin[t, s] = total.astype(BF16)
            for m in range(1, tp):
                last.append(send(fin.at[t, s], fin.at[t, s], o_s.at[s, m], o_r.at[s, m], tensor=(t + m) % tp))
                last[-1].start()
    pending += reduced.values()
    pending += last
    for copy in last:
        copy.wait_recv()
    for c in range(tp):
        for s in range(split):
            out[:, (c * split + s) * part : (c * split + s + 1) * part] = fin[c, s]
    for copy in pending:
        copy.wait_send()

    @pl.when(mine)
    def _shared():
        for copy in shares:
            copy.wait_send()


def local(
    dp, tp, residual, query_latent, query_rope, cache_latent, cache_rope, lengths, value_up, out_proj,
    gate_proj, up_proj, down_proj, groups, expert_picks, gate_levels,
):
    row_n, model = residual.shape
    per_group = dp // min(8, dp // 2)
    rows = dp * row_n
    depth, cols = out_proj.shape
    units = gate_proj.shape[2]
    heads, lat = query_latent.shape[1:]
    quarter = rows // tp
    split = 2
    part = model // (tp * split)
    count = tp * split
    chips = dp // 2
    step_rows = 4
    vm = lambda *shape: pltpu.VMEM(shape, BF16)
    wide = lambda *shape: pltpu.VMEM(shape, F32)
    sem = lambda *shape: pltpu.SemaphoreType.DMA(shape)
    hidden, routed = pl.pallas_call(
        functools.partial(layer_kernel, dp, tp, per_group),
        out_shape=[jax.ShapeDtypeStruct((row_n, model), BF16)] * 2,
        in_specs=[pl.BlockSpec(memory_space=pltpu.SMEM)]
        + [pl.BlockSpec(memory_space=pltpu.VMEM)] * 4
        + [pl.BlockSpec(memory_space=pl.ANY)] * 9,
        out_specs=[pl.BlockSpec(memory_space=pltpu.VMEM)] * 2,
        scratch_shapes=[
            vm(*query_latent.shape), vm(*query_rope.shape),
            vm(2, step_rows, *cache_latent.shape[1:]), vm(2, step_rows, *cache_rope.shape[1:]),
            vm(*value_up.shape), wide(row_n, heads, lat),
            vm(depth, cols), vm(model, units), vm(model, units), vm(units, model),
            vm(dp, row_n, cols), vm(2, dp, row_n, depth // 2), wide(dp, row_n, 128),
            vm(dp // tp, row_n, cols),
            wide(tp, quarter, cols), vm(tp, quarter, cols), vm(tp, quarter, cols),
            vm(dp, rows, cols), wide(rows, units), wide(rows, units),
            vm(count, 2, chips, row_n, part), vm(count, chips, row_n, part),
            vm(count, chips - 1, row_n, part), vm(count, row_n, part), vm(count, row_n, part),
            vm(tp, split, row_n, part),
            sem(2), sem(2), sem(7), sem(dp), sem(dp), sem(2, chips), sem(2, chips), sem(2, chips), sem(2, chips),
            sem(dp), sem(dp // tp), sem(tp), sem(tp), sem(tp), sem(tp),
            sem(tp, chips), sem(tp, chips), sem(tp, chips), sem(tp, chips),
            sem(count), sem(count), sem(count, chips), sem(count, chips), sem(count), sem(count),
            sem(split, tp), sem(split, tp),
        ],
        compiler_params=pltpu.CompilerParams(
            collective_id=0, has_side_effects=True, vmem_limit_bytes=60 * MIB
        ),
        cost_estimate=pl.CostEstimate(
            flops=2 * rows * (depth * cols + 3 * model * units) + 2 * row_n * heads * 1024 * 1088,
            bytes_accessed=42 * MIB, transcendentals=0,
        ),
    )(
        lengths, residual, groups.T, expert_picks.T, gate_levels.T, query_latent, query_rope,
        cache_latent, cache_rope, value_up, out_proj, gate_proj, up_proj, down_proj,
    )
    return (hidden.astype(F32) + routed.astype(F32)).astype(BF16)


def solution(mesh):
    return jax.shard_map(
        functools.partial(local, mesh.shape["dp"], mesh.shape["tensor"]),
        mesh=mesh,
        in_specs=(
            P("dp", None),
            P("dp", "tensor", None),
            P("dp", "tensor", None),
            P("dp", None, None),
            P("dp", None, None),
            P("dp"),
            P("tensor", None, None),
            P("tensor", "dp"),
            P("dp", None, "tensor"),
            P("dp", None, "tensor"),
            P("dp", "tensor", None),
            P("dp", None),
            P("dp", None),
            P("dp", None),
        ),
        out_specs=P("dp", None),
        check_vma=False,
    )
```

```python
import functools

import jax
import jax.numpy as jnp
from jax import lax
from jax.experimental import pallas as pl
from jax.experimental.pallas import tpu as pltpu
from jax.sharding import PartitionSpec as P

score_scale = 192.0 ** (-0.5)
route_scale = 2.5
far_below = -1e30
MIB = 1 << 20
F32 = jnp.float32
BF16 = jnp.bfloat16


def flip(index, mask, size):
    out, bit = 0, 1
    while bit < size:
        here = index // bit % 2
        out = out + bit * ((here + 1) % 2 if mask & bit else here)
        bit *= 2
    return out


def gate_table(owners, per_group, groups, picks, levels):
    rows = picks.shape[1]
    level = levels[...].astype(F32)
    gates = route_scale * level / jnp.sum(level, axis=0, keepdims=True)
    group = groups[...]
    pick = picks[...]
    expert = pick
    for s in range(group.shape[0]):
        inside = (pick >= s * per_group) & (pick < (s + 1) * per_group)
        expert = jnp.where(inside, pick + (group[s : s + 1, :] - s) * per_group, expert)
    same = lax.broadcasted_iota(jnp.int32, (rows, rows), 0) == lax.broadcasted_iota(jnp.int32, (rows, rows), 1)
    lane = lax.broadcasted_iota(jnp.int32, (rows, 128), 1)
    total = jnp.zeros((rows, 128), F32)
    for e in range(owners):
        along = jnp.sum(jnp.where(expert == e, gates, 0.0), axis=0, keepdims=True)
        down = jnp.sum(jnp.where(same, along, 0.0), axis=1, keepdims=True)
        total += jnp.where(lane == e, down, 0.0)
    return total


def layer_kernel(
    dp, tp, per_group, lengths, resid, groups, picks, levels,
    ql_h, qr_h, cl_h, cr_h, vu_h, wo_h, wg_h, wu_h, wd_h, hid_out, out,
    ql, qr, cl, cr, vu, mix, wo, wg, wu, wd, rblk, hbuf, cbuf, resb, acc, pbuf, rbuf, hid,
    accg, accu, pd, sr, xr, zs, zr, fin,
    l_sem, r_sem, w_sem, c_s, c_r, a_s, a_r, f_s, f_r, q_s, q_r, b_s, b_r, z_s, z_r, x_s, x_r, y_s, y_r,
    d_s, d_r, e_s, e_r, g_s, g_r, o_s, o_r,
):
    d = lax.axis_index("dp")
    t = lax.axis_index("tensor")
    chips = dp // 2
    chip, core = d // 2, d % 2
    sib = chip * 2 + (1 - core)
    row_n = resid.shape[0]
    rows = dp * row_n
    quarter = rows // tp
    depth, cols = wo.shape
    per_quarter = dp // tp
    near_first = list(range(1, chips))
    far_first = near_first[::-1]
    steps = row_n // cl.shape[1]
    step_rows = cl.shape[1]
    heads, positions = ql.shape[1], cl.shape[2]
    width = vu.shape[2]
    rope = qr.shape[2]
    parts = hbuf.shape[0]
    chunk = depth // parts

    def send(src, dst, ss, rs, **where):
        return pltpu.make_async_remote_copy(
            src_ref=src, dst_ref=dst, send_sem=ss, recv_sem=rs,
            device_id=where, device_id_type=pl.DeviceIdType.MESH,
        )

    def over(mask):
        return flip(chip, mask, chips) * 2 + core

    barrier = pltpu.get_barrier_semaphore()
    for k in range(1, dp):
        pl.semaphore_signal(barrier, inc=1, device_id={"dp": (d + k) % dp}, device_id_type=pl.DeviceIdType.MESH)
    for k in range(1, tp):
        pl.semaphore_signal(barrier, inc=1, device_id={"tensor": (t + k) % tp}, device_id_type=pl.DeviceIdType.MESH)

    def fetch(step, slot):
        at = pl.ds(step * step_rows, step_rows)
        return (
            pltpu.make_async_copy(cl_h.at[at], cl.at[slot], l_sem.at[slot]),
            pltpu.make_async_copy(cr_h.at[at], cr.at[slot], r_sem.at[slot]),
        )

    loads = [
        pltpu.make_async_copy(src, dst, w_sem.at[i])
        for i, (src, dst) in enumerate((
            (wo_h, wo), (wg_h.at[0], wg), (wu_h.at[0], wu), (wd_h.at[0], wd), (vu_h, vu), (ql_h, ql), (qr_h, qr),
        ))
    ]
    loads[5].start()
    loads[6].start()
    for copy in fetch(0, 0):
        copy.start()
    for j in range(dp):
        rblk[j] = resid[:, j * cols : (j + 1) * cols]
    cbuf[d] = gate_table(dp, per_group, groups, picks, levels)
    loads[5].wait()
    loads[6].wait()

    @pl.loop(0, steps)
    def _attend(step):
        slot = step % 2

        @pl.when(step + 1 < steps)
        def _next():
            for copy in fetch(step + 1, 1 - slot):
                copy.start()

        @pl.when(step == 0)
        def _later():
            loads[4].start()
            loads[0].start()

        for copy in fetch(step, slot):
            copy.wait()
        place = lax.broadcasted_iota(jnp.int32, (heads, positions), 1)
        base = step * step_rows
        span = range(step_rows)
        ropes = qr[pl.ds(base, step_rows)].reshape(step_rows * heads, rope)
        spread_q = jnp.concatenate([ropes] * step_rows, axis=1)
        from_row = lax.broadcasted_iota(jnp.int32, spread_q.shape, 0) // heads
        to_row = lax.broadcasted_iota(jnp.int32, spread_q.shape, 1) // rope
        spread_q = jnp.where(from_row == to_row, spread_q.astype(F32), 0.0).astype(BF16)
        keys = cr[slot].reshape(step_rows * rope, positions)
        rope_scores = jnp.dot(spread_q, keys, preferred_element_type=F32)
        scores = [
            lax.dot_general(ql[base + i], cl[slot, i], (((1,), (1,)), ((), ())), preferred_element_type=F32)
            + rope_scores[i * heads : (i + 1) * heads, :]
            for i in span
        ]
        scores = [jnp.where(place < lengths[base + i], scores[i] * score_scale, far_below) for i in span]
        highest = [jnp.max(scores[i], axis=1, keepdims=True) for i in span]
        raised = [jnp.exp(scores[i] - highest[i]) for i in span]
        totals = [jnp.sum(raised[i], axis=1, keepdims=True) for i in span]
        for i in span:
            mix[base + i] = jnp.dot(raised[i].astype(BF16), cl[slot, i], preferred_element_type=F32) / totals[i]

    for i in (1, 2, 3):
        loads[i].start()
    pl.semaphore_wait(barrier, dp - 1 + tp - 1)
    pending = []

    coefs = []
    for k in range(1, dp):
        coefs.append(send(cbuf.at[d], cbuf.at[d], c_s.at[k], c_r.at[k], dp=(d + k) % dp))
        coefs[-1].start()
    pending += coefs

    mine = d // per_quarter == t
    slot = d % per_quarter
    shares = [
        send(rblk.at[(d + k) % dp], resb.at[slot], q_s.at[k], q_r.at[slot], dp=(d + k) % dp)
        for k in range(1, dp)
    ]

    @pl.when(mine)
    def _share():
        for copy in shares:
            copy.start()
        resb[slot] = rblk[d]

    loads[4].wait()
    gather = {}
    for p in range(parts):
        for h in range(p * heads // parts, (p + 1) * heads // parts, 2):
            mixed = jnp.concatenate([mix[:, h, :], mix[:, h + 1, :]], axis=0).astype(BF16)
            both = jnp.concatenate([vu[h], vu[h + 1]], axis=1)
            value = jnp.dot(mixed, both, preferred_element_type=F32).astype(BF16)
            at = h * width - p * chunk
            hbuf[p, d, :, at : at + width] = value[:row_n, :width]
            hbuf[p, d, :, at + width : at + 2 * width] = value[row_n:, width:]
        block = hbuf.at[p, d]
        for j in near_first + [0]:
            gather[p, j] = send(block, block, a_s.at[p, j], a_r.at[p, j], dp=over(j) if j else sib)
            gather[p, j].start()
    pending += gather.values()
    loads[0].wait()

    forwards = {}
    for p in range(parts):
        for j in near_first:
            gather[p, j].wait_recv()
            block = hbuf.at[p, over(j)]
            forwards[p, j] = send(block, block, f_s.at[p, j], f_r.at[p, j], dp=sib)
            forwards[p, j].start()
        gather[p, 0].wait_recv()
        for j in near_first:
            forwards[p, j].wait_recv()
        fine = min(512, chunk)
        if p == 0:
            acc[...] = jnp.zeros_like(acc)

        @pl.loop(0, chunk // fine)
        def _project(k):
            at = pl.ds(pl.multiple_of(k * fine, fine), fine)
            down = pl.ds(pl.multiple_of(p * chunk + k * fine, fine), fine)
            acc[...] += jnp.dot(
                hbuf[p, :, :, at].reshape(rows, fine), wo[down, :], preferred_element_type=F32
            ).reshape(acc.shape)

    pending += forwards.values()
    pbuf[...] = acc[...].astype(BF16)
    sums = []
    for k in range(1, tp):
        u = (t + k) % tp
        sums.append(send(pbuf.at[u], rbuf.at[k], b_s.at[k], b_r.at[k], tensor=u))
        sums[-1].start()
    pending += sums
    for i in range(per_quarter):
        owner = t * per_quarter + i

        @pl.when(owner != d)
        def _arrive():
            send(rblk.at[0], resb.at[i], q_s.at[0], q_r.at[i], dp=owner).wait_recv()

    my_rows = pl.ds(pl.multiple_of(t * quarter, quarter), quarter)
    piece = acc[t]
    for k in range(1, tp):
        sums[k - 1].wait_recv()
        piece += rbuf[k].astype(F32)
    attention = piece.astype(BF16).astype(F32)
    hid[d, my_rows, :] = (attention + resb[...].reshape(quarter, cols).astype(F32)).astype(BF16)

    along = []
    for k in range(1, tp):
        along.append(send(hid.at[d, my_rows], hid.at[d, my_rows], z_s.at[k], z_r.at[k], tensor=(t + k) % tp))
        along[-1].start()
    pending += along
    spread = {}
    for k in range(tp):
        if k:
            along[k - 1].wait_recv()
        at = pl.ds(pl.multiple_of((t + tp - k) % tp * quarter, quarter), quarter)
        for j in near_first:
            spread[k, j] = send(hid.at[d, at], hid.at[d, at], x_s.at[k, j], x_r.at[k, j], dp=over(j))
            spread[k, j].start()
        spread[k, 0] = send(hid.at[d, at], hid.at[d, at], x_s.at[k, 0], x_r.at[k, 0], dp=sib)
        spread[k, 0].start()
    pending += spread.values()

    loads[1].wait()
    loads[2].wait()
    accg[...] = jnp.zeros_like(accg)
    accu[...] = jnp.zeros_like(accu)

    def expand(block):
        at = pl.ds(pl.multiple_of(block * cols, cols), cols)
        values = hid[block]
        accg[...] += jnp.dot(values, wg[at, :], preferred_element_type=F32)
        accu[...] += jnp.dot(values, wu[at, :], preferred_element_type=F32)

    expand(d)
    passed = {}
    for k in range(tp):
        if k == tp - 1:
            for m in range(tp):
                spread[m, 0].wait_recv()
            expand(sib)
        at = pl.ds(pl.multiple_of((t + tp - k) % tp * quarter, quarter), quarter)
        for j in near_first:
            spread[k, j].wait_recv()
            block = over(j)
            passed[k, j] = send(hid.at[block, at], hid.at[block, at], y_s.at[k, j], y_r.at[k, j], dp=sib)
            passed[k, j].start()
    pending += passed.values()

    @pl.loop(0, chips - 1)
    def _same(j):
        expand((chip + 1 + j) % chips * 2 + core)

    for copy in passed.values():
        copy.wait_recv()

    @pl.loop(0, chips - 1)
    def _other(j):
        expand((chip + 1 + j) % chips * 2 + 1 - core)

    for copy in coefs:
        copy.wait_recv()
    table = cbuf[...].reshape(rows, 128)
    lane = lax.broadcasted_iota(jnp.int32, (rows, 128), 1)
    weight = jnp.sum(jnp.where(lane == d, table, 0.0), axis=1, keepdims=True)
    gated = accg[...]
    active = (gated / (1.0 + jnp.exp(-gated)) * accu[...] * weight).astype(BF16)

    loads[3].wait()
    split, part = fin.shape[1], fin.shape[3]
    pieces = [(s, k) for s in range(split) for k in list(range(1, tp)) + [0]]
    halves = []
    across = {}

    def cross(n):
        halves[n].wait_recv()
        pd[n, core] = (pd[n, core].astype(F32) + sr[n].astype(F32)).astype(BF16)
        for j in far_first:
            peer = flip(chip, j, chips)
            across[n, j] = send(pd.at[n, core, peer], xr.at[n, j - 1], e_s.at[n, j], e_r.at[n, j], dp=peer * 2 + core)
            across[n, j].start()

    for n, (s, k) in enumerate(pieces):
        at = pl.ds(pl.multiple_of(((t + k) % tp * split + s) * part, part), part)
        produced = jnp.dot(active, wd[:, at], preferred_element_type=F32).astype(BF16)
        for b in range(dp):
            pd[n, b % 2, b // 2] = produced[b * row_n : (b + 1) * row_n, :]
        halves.append(send(pd.at[n, 1 - core], sr.at[n], d_s.at[n], d_r.at[n], dp=sib))
        halves[-1].start()
        if n >= 2:
            cross(n - 2)
    cross(len(pieces) - 2)
    cross(len(pieces) - 1)
    pending += halves
    pending += across.values()
    own_rows = pl.ds(pl.multiple_of(d * row_n, row_n), row_n)
    for b in range(dp):
        hid_out[:, b * cols : (b + 1) * cols] = hid[b, own_rows, :]
    reduced = {}
    last = []
    for n, (s, k) in enumerate(pieces):
        total = pd[n, core, chip].astype(F32)
        for j in far_first:
            across[n, j].wait_recv()
            total += xr[n, j - 1].astype(F32)
        if k:
            zs[n] = total.astype(BF16)
            reduced[s, k] = send(zs.at[n], zr.at[n], g_s.at[n], g_r.at[n], tensor=(t + k) % tp)
            reduced[s, k].start()
        else:
            for m in range(1, tp):
                reduced[s, m].wait_recv()
                total += zr[s * tp + m - 1].astype(F32)
            fin[t, s] = total.astype(BF16)
            for m in range(1, tp):
                last.append(send(fin.at[t, s], fin.at[t, s], o_s.at[s, m], o_r.at[s, m], tensor=(t + m) % tp))
                last[-1].start()
    pending += reduced.values()
    pending += last
    for copy in last:
        copy.wait_recv()
    for c in range(tp):
        for s in range(split):
            out[:, (c * split + s) * part : (c * split + s + 1) * part] = fin[c, s]
    for copy in pending:
        copy.wait_send()

    @pl.when(mine)
    def _shared():
        for copy in shares:
            copy.wait_send()


def local(
    dp, tp, residual, query_latent, query_rope, cache_latent, cache_rope, lengths, value_up, out_proj,
    gate_proj, up_proj, down_proj, groups, expert_picks, gate_levels,
):
    row_n, model = residual.shape
    per_group = dp // min(8, dp // 2)
    rows = dp * row_n
    depth, cols = out_proj.shape
    units = gate_proj.shape[2]
    heads, lat = query_latent.shape[1:]
    quarter = rows // tp
    split = 2
    part = model // (tp * split)
    count = tp * split
    chips = dp // 2
    step_rows = 4
    vm = lambda *shape: pltpu.VMEM(shape, BF16)
    wide = lambda *shape: pltpu.VMEM(shape, F32)
    sem = lambda *shape: pltpu.SemaphoreType.DMA(shape)
    hidden, routed = pl.pallas_call(
        functools.partial(layer_kernel, dp, tp, per_group),
        out_shape=[jax.ShapeDtypeStruct((row_n, model), BF16)] * 2,
        in_specs=[pl.BlockSpec(memory_space=pltpu.SMEM)]
        + [pl.BlockSpec(memory_space=pltpu.VMEM)] * 4
        + [pl.BlockSpec(memory_space=pl.ANY)] * 9,
        out_specs=[pl.BlockSpec(memory_space=pltpu.VMEM)] * 2,
        scratch_shapes=[
            vm(*query_latent.shape), vm(*query_rope.shape),
            vm(2, step_rows, *cache_latent.shape[1:]), vm(2, step_rows, *cache_rope.shape[1:]),
            vm(*value_up.shape), wide(row_n, heads, lat),
            vm(depth, cols), vm(model, units), vm(model, units), vm(units, model),
            vm(dp, row_n, cols), vm(2, dp, row_n, depth // 2), wide(dp, row_n, 128),
            vm(dp // tp, row_n, cols),
            wide(tp, quarter, cols), vm(tp, quarter, cols), vm(tp, quarter, cols),
            vm(dp, rows, cols), wide(rows, units), wide(rows, units),
            vm(count, 2, chips, row_n, part), vm(count, chips, row_n, part),
            vm(count, chips - 1, row_n, part), vm(count, row_n, part), vm(count, row_n, part),
            vm(tp, split, row_n, part),
            sem(2), sem(2), sem(7), sem(dp), sem(dp), sem(2, chips), sem(2, chips), sem(2, chips), sem(2, chips),
            sem(dp), sem(dp // tp), sem(tp), sem(tp), sem(tp), sem(tp),
            sem(tp, chips), sem(tp, chips), sem(tp, chips), sem(tp, chips),
            sem(count), sem(count), sem(count, chips), sem(count, chips), sem(count), sem(count),
            sem(split, tp), sem(split, tp),
        ],
        compiler_params=pltpu.CompilerParams(
            collective_id=0, has_side_effects=True, vmem_limit_bytes=60 * MIB
        ),
        cost_estimate=pl.CostEstimate(
            flops=2 * rows * (depth * cols + 3 * model * units) + 2 * row_n * heads * 1024 * 1088,
            bytes_accessed=42 * MIB, transcendentals=0,
        ),
    )(
        lengths, residual, groups.T, expert_picks.T, gate_levels.T, query_latent, query_rope,
        cache_latent, cache_rope, value_up, out_proj, gate_proj, up_proj, down_proj,
    )
    return (hidden.astype(F32) + routed.astype(F32)).astype(BF16)


def solution(mesh):
    return jax.shard_map(
        functools.partial(local, mesh.shape["dp"], mesh.shape["tensor"]),
        mesh=mesh,
        in_specs=(
            P("dp", None),
            P("dp", "tensor", None),
            P("dp", "tensor", None),
            P("dp", None, None),
            P("dp", None, None),
            P("dp"),
            P("tensor", None, None),
            P("tensor", "dp"),
            P("dp", None, "tensor"),
            P("dp", None, "tensor"),
            P("dp", "tensor", None),
            P("dp", None),
            P("dp", None),
            P("dp", None),
        ),
        out_specs=P("dp", None),
        check_vma=False,
    )
```
